32 devices in a mesh: cells: 8 (over z, y), per: 4 (over x, core).
Axes of the slice: x: 2, y: 2, z: 4, core: 2. Of those that a mesh axis runs over, the one named last changes fastest.
Arguments:
- field: float32 [128, 2, 8, 4096], P('per', None, None, 'cells'), may hold values from -12 to 12
- period_gain: float32 [128], replicated, may hold values from 0.3 to 3
- start_basis: float32 [128, 32], replicated, may hold values from -0.5 to 0.5
Outputs:
- projected: float32 [128, 2, 8, 4096], P('per', None, None, 'cells')
The draws below stay inside these ranges and needn't reach their ends.
All inputs are finite; a program needn't handle non-finite values.
Results may differ from the reference program's by a relative error of at most 0.0003.
Values sent between devices are 32-bit elements; how exact they have to be, the bound alone decides.
A program may use at most 192 MiB of HBM per device.

```python
import math
import jax
import jax.numpy as jnp
from jax import lax

PERIODS = 128
RANK = 32
LAYERS = 8
ITERS = 3
CELLS = 4096


def draw_field(key, part):
    key = jax.random.fold_in(key, 11)
    first = jax.random.fold_in(key, 0)
    second = jax.random.fold_in(key, 1)
    fourth = jax.random.fold_in(key, 3)
    fifth = jax.random.fold_in(key, 4)
    shape = (PERIODS, 2, LAYERS, CELLS)
    ramp = jnp.exp(jnp.log(3.0) * jnp.arange(CELLS, dtype=jnp.float32) / max(CELLS - 1, 1))
    rough = jnp.exp(jax.random.uniform(second, (CELLS,), minval=-0.7, maxval=0.7))
    position = (jnp.arange(PERIODS, dtype=jnp.float32) + 0.5) / PERIODS
    phases = jax.random.uniform(fourth, (16,), minval=0.0, maxval=2.0 * math.pi)
    weights = jax.random.normal(fifth, (16, 2, LAYERS, CELLS))
    common = jnp.zeros(shape, jnp.float32)
    for index in range(16):
        profile = jnp.cos(math.pi * (index + 0.5) * position + phases[index]) * math.sqrt(2.0 / 16.0)
        common = common + profile[:, None, None, None] * weights[index][None]
    base = jax.random.normal(first, shape)
    values = (base + common) * ramp * rough
    return jnp.clip(values, -12.0, 12.0).astype(jnp.float32)


def scatter_about(own_key, shape, scale, reach, kind=jnp.bfloat16):
    return jnp.clip(scale * jax.random.normal(own_key, shape, jnp.float32), -reach, reach).astype(kind)


def setup_inputs(seed: int = 0) -> dict:
    seeds = jax.random.split(jax.random.key(seed), 4)
    return {
        "field": draw_field(jax.random.fold_in(seeds[3], 71), 0),
        "period_gain": jnp.clip(jnp.exp(jax.random.uniform(seeds[1], (PERIODS,), jnp.float32, math.log(0.3), math.log(3.0))), 0.3, 3.0),
        "start_basis": scatter_about(seeds[2], (PERIODS, RANK), PERIODS ** -0.5, 0.5, jnp.float32),
    }


HIGH = lax.Precision.HIGHEST

def refine(gram, basis):
    for step in range(ITERS):
        grown = jnp.dot(gram, basis, precision=HIGH)
        inner = jnp.dot(grown.T, grown, precision=HIGH)
        lower = jnp.linalg.cholesky(inner)
        basis = lax.linalg.triangular_solve(lower, grown, left_side=False, lower=True, transpose_a=True)
    return basis

def reference(field, period_gain, start_basis):
    scaled = field * period_gain[:, None, None, None]
    flat = scaled.reshape(scaled.shape[0], -1)
    gram = lax.dot_general(flat, flat, (((1,), (1,)), ((), ())), precision=HIGH) / (2.0 * LAYERS * CELLS)
    basis = refine(gram, start_basis)
    projector = jnp.dot(basis, basis.T, precision=HIGH)
    result = lax.dot_general(projector, flat, (((0,), (0,)), ((), ())), precision=HIGH)
    return result.reshape(scaled.shape)
```

```python
import functools
import jax
import jax.numpy as jnp
from jax import lax
from jax.experimental import pallas as pl
from jax.experimental.pallas import tpu as pltpu
from jax.sharding import PartitionSpec as P

ITERS = 3
HIGH = lax.Precision.HIGHEST
MESH = pl.DeviceIdType.MESH
F32 = jnp.float32
BF16 = jnp.bfloat16


def split_two(x):
    hi = x.astype(BF16)
    return hi, (x - hi.astype(F32)).astype(BF16)


def refine_step(gram, basis_t):
    rank, periods = basis_t.shape
    grown = jnp.dot(basis_t, gram, precision=HIGH, preferred_element_type=F32)
    inner = lax.dot_general(grown, grown, (((1,), (1,)), ((), ())), precision=HIGH,
                            preferred_element_type=F32)
    row_id = lax.broadcasted_iota(jnp.int32, (rank, 1), 0)
    for k in range(rank - 1):
        below = jnp.where(row_id > k, inner[:, k:k + 1], 0.0)
        inverse = 1.0 / inner[k:k + 1, k:k + 1]
        grown_row = grown[k:k + 1, :] * inverse
        inner_row = inner[k:k + 1, :] * inverse
        grown = grown - below * grown_row
        inner = inner - below * inner_row
    eye = lax.broadcasted_iota(jnp.int32, (rank, rank), 0) == lax.broadcasted_iota(
        jnp.int32, (rank, rank), 1)
    pivots = jnp.sum(jnp.where(eye, inner, 0.0), axis=1, keepdims=True)
    return grown * lax.rsqrt(pivots)


def kernel(cells, total_rows, field, gain_ref, start_ref, out, buf, parts, out_buf, gram_part,
           scattered, slots, gram_full, proj_ref, local_sem, out_sem, send1, recv1, send2, recv2,
           relay_send, relay_recv, rs_send, rs_recv, bc_send, bc_recv, ag_send, ag_recv):
    me = lax.axis_index("per")
    my_cell = lax.axis_index("cells")
    sib = me + 1 - 2 * lax.rem(me, 2)
    peer = lax.rem(me + 2, 4)
    cross = lax.rem(sib + 2, 4)
    base = 2 * (1 - me // 2)
    others = (sib, peer, cross)
    own = field.shape[0]
    layers = field.shape[2]
    rows = 2 * layers

    def lanes(j):
        return pl.ds(pl.multiple_of(j * 128, 128), 128)

    local = []
    for index, j in enumerate((me,) + others):
        copy = pltpu.make_async_copy(field.at[:, :, :, lanes(j)], buf.at[j, me], local_sem.at[index])
        copy.start()
        local.append(copy)

    barrier = pltpu.get_barrier_semaphore()
    for other in others:
        pl.semaphore_signal(barrier, inc=1, device_id={"per": other}, device_id_type=MESH)

    def greet(step, carry):
        pl.semaphore_signal(barrier, inc=1, device_id={"cells": lax.rem(my_cell + step, cells)},
                            device_id_type=MESH)
        return carry

    lax.fori_loop(1, cells, greet, 0)
    pl.semaphore_wait(barrier, 3 + cells - 1)

    def remote(src, dst, send, recv, other):
        return pltpu.make_async_remote_copy(src_ref=src, dst_ref=dst, send_sem=send, recv_sem=recv,
                                            device_id={"per": other}, device_id_type=MESH)

    first = {}
    for a in range(2):
        for rel in (1, 2, 0):
            other = others[rel]
            copy = remote(field.at[:, a, :, lanes(other)], buf.at[other, me, :, a],
                          send1.at[rel, a], recv1.at[rel, a], other)
            copy.start()
            first[rel, a] = copy

    second = []
    for index, j in enumerate((me, peer, cross)):
        copy = remote(field.at[:, :, :, lanes(j)], buf.at[j, me], send2.at[index], recv2.at[index], sib)
        copy.start()
        second.append(copy)

    gain_row = gain_ref[...]
    gain_col = jnp.broadcast_to(gain_row, (128, 128)).T
    basis_t = start_ref[...].T

    acc = jnp.zeros((256, 256), F32)
    for copy in local:
        copy.wait()
    mine = buf.at[me].reshape(128 * rows, 128)
    for a in range(2):
        for rel in range(3):
            first[rel, a].wait_recv()
        for pair in range(layers // 2):
            block = []
            for l in (2 * pair, 2 * pair + 1):
                x = mine[pl.ds(a * layers + l, 128, stride=rows), :]
                hi, lo = split_two(x)
                y = jnp.concatenate([hi, lo], axis=0)
                parts[me, a * layers + l] = y
                block.append(y)
            both = jnp.concatenate(block, axis=1)
            acc = acc + lax.dot_general(both, both, (((1,), (1,)), ((), ())),
                                        preferred_element_type=F32)
    gram_part[...] = (acc[:128, :128] + acc[128:, 128:]) + (acc[:128, 128:] + acc[128:, :128])

    def own_rows(g):
        return pl.ds(pl.multiple_of(g * own, own), own)

    scatter = []
    for rel in (1, 2, 0):
        copy = remote(gram_part.at[own_rows(others[rel])], scattered.at[rel], rs_send.at[rel],
                      rs_recv.at[rel], others[rel])
        copy.start()
        scatter.append(copy)
    relay_a = remote(buf.at[me, pl.ds(base, 2)], buf.at[me, pl.ds(base, 2)], relay_send.at[0],
                     relay_recv.at[0], sib)
    relay_a.start()
    for copy in scatter:
        copy.wait_recv()
    slots[my_cell] = (gram_part[own_rows(me), :] + scattered[0]) + (scattered[1] + scattered[2])

    def broadcast(step):
        other = lax.rem(my_cell + step, cells)
        return pltpu.make_async_remote_copy(
            src_ref=slots.at[my_cell], dst_ref=slots.at[my_cell], send_sem=bc_send.at[other],
            recv_sem=bc_recv.at[my_cell], device_id={"cells": other}, device_id_type=MESH)

    def arrival(step):
        other = lax.rem(my_cell + step, cells)
        return pltpu.make_async_remote_copy(
            src_ref=slots.at[other], dst_ref=slots.at[other], send_sem=bc_send.at[other],
            recv_sem=bc_recv.at[other], device_id={"cells": other}, device_id_type=MESH)

    def start_broadcast(step, carry):
        broadcast(step).start()
        return carry

    def wait_broadcast(step, carry):
        arrival(step).wait_recv()
        return carry

    def wait_sent(step, carry):
        broadcast(step).wait_send()
        return carry

    lax.fori_loop(1, cells, start_broadcast, 0)

    across = []
    for rel, j in ((1, me), (2, sib)):
        copy = remote(field.at[:, :, :, lanes(j)], buf.at[j, me], send2.at[2 + rel], recv2.at[2 + rel],
                      others[rel])
        copy.start()
        across.append(copy)

    def prepare(j, g):
        source = buf.at[j, g].reshape(own * rows, 128)
        for r in range(rows):
            hi, lo = split_two(source[pl.ds(r, own, stride=rows), :])
            parts[j, r, own_rows(g), :] = hi
            parts[j, r, pl.ds(pl.multiple_of(128 + g * own, own), own), :] = lo

    for j in (sib, peer, cross):
        prepare(j, me)
    for copy in second:
        copy.wait_recv()
    for j in (sib, peer, cross):
        prepare(j, sib)

    lax.fori_loop(1, cells, wait_broadcast, 0)

    def add(step, total):
        return total + slots[step]

    gram_full[own_rows(me), :] = lax.fori_loop(1, cells, add, slots[0])
    gather = []
    for rel in (1, 2, 0):
        copy = remote(gram_full.at[own_rows(me)], gram_full.at[own_rows(me)], ag_send.at[rel],
                      ag_recv.at[rel], others[rel])
        copy.start()
        gather.append(copy)
    for copy in gather:
        copy.wait_recv()

    gram = gram_full[...] * gain_row * gain_col * (1.0 / total_rows)
    basis_t = lax.fori_loop(0, ITERS - 1, lambda step, b: refine_step(gram, b), basis_t)

    for copy in across:
        copy.wait_recv()
    relay_b = remote(buf.at[peer, pl.ds(base, 2)], buf.at[peer, pl.ds(base, 2)], relay_send.at[1],
                     relay_recv.at[1], sib)
    relay_b.start()
    basis_t = refine_step(gram, basis_t)
    proj_ref[...] = lax.dot_general(basis_t, basis_t, (((0,), (0,)), ((), ())), precision=HIGH,
                                    preferred_element_type=F32)
    hi, lo = split_two(proj_ref[own_rows(me), :] * gain_row)
    weights = jnp.concatenate([jnp.concatenate([hi, hi], axis=1),
                               jnp.concatenate([lo, jnp.zeros_like(lo)], axis=1)], axis=0)

    relay_a.wait_recv()
    for g in (peer, cross):
        prepare(peer, g)
        prepare(sib, g)
    relay_b.wait_recv()
    for g in (peer, cross):
        prepare(cross, g)

    written = []
    for index, j in enumerate((me,) + others):
        target = out_buf.at[j].reshape(own * rows, 128)
        for r in range(0, rows, 2):
            both = jnp.concatenate([parts[j, r], parts[j, r + 1]], axis=1)
            result = jnp.dot(weights, both, preferred_element_type=F32)
            result = result[:own] + result[own:]
            target[pl.ds(r, own, stride=rows), :] = result[:, :128]
            target[pl.ds(r + 1, own, stride=rows), :] = result[:, 128:]
        copy = pltpu.make_async_copy(out_buf.at[j], out.at[:, :, :, lanes(j)], out_sem.at[index])
        copy.start()
        written.append(copy)

    for copy in list(first.values()) + second + across + scatter + gather + [relay_a, relay_b]:
        copy.wait_send()
    lax.fori_loop(1, cells, wait_sent, 0)
    for copy in written:
        copy.wait()


def per_device(field, period_gain, start_basis):
    cells = lax.axis_size("cells")
    own, _, layers, width = field.shape
    total_rows = 2.0 * layers * width * cells
    any_space = pl.BlockSpec(memory_space=pl.ANY)
    vmem = pl.BlockSpec(memory_space=pltpu.VMEM)
    dma = pltpu.SemaphoreType.DMA
    return pl.pallas_call(
        functools.partial(kernel, cells, total_rows),
        out_shape=jax.ShapeDtypeStruct(field.shape, F32),
        in_specs=[any_space, vmem, vmem],
        out_specs=any_space,
        scratch_shapes=[
            pltpu.VMEM((4, 4, own, 2, layers, 128), F32),
            pltpu.VMEM((4, 2 * layers, 256, 128), BF16),
            pltpu.VMEM((4, own, 2, layers, 128), F32),
            pltpu.VMEM((128, 128), F32),
            pltpu.VMEM((3, own, 128), F32),
            pltpu.VMEM((cells, own, 128), F32),
            pltpu.VMEM((128, 128), F32),
            pltpu.VMEM((128, 128), F32),
            dma((4,)), dma((4,)),
            dma((3, 2)), dma((3, 2)),
            dma((5,)), dma((5,)),
            dma((2,)), dma((2,)),
            dma((3,)), dma((3,)),
            dma((cells,)), dma((cells,)),
            dma((3,)), dma((3,)),
        ],
        compiler_params=pltpu.CompilerParams(
            collective_id=0, has_side_effects=True, vmem_limit_bytes=40 * 1024 * 1024),
        name="factor_and_project",
    )(field, period_gain.reshape(1, -1), start_basis)


def solution(mesh):
    in_specs = (P("per", None, None, "cells"), P(), P())
    out_specs = P("per", None, None, "cells")
    return jax.shard_map(
        per_device, mesh=mesh, in_specs=in_specs, out_specs=out_specs, check_vma=False
    )
```

```python
import functools
import jax
import jax.numpy as jnp
from jax import lax
from jax.experimental import pallas as pl
from jax.experimental.pallas import tpu as pltpu
from jax.sharding import PartitionSpec as P

ITERS = 3
HIGH = lax.Precision.HIGHEST
MESH = pl.DeviceIdType.MESH
F32 = jnp.float32
BF16 = jnp.bfloat16


def split_two(x):
    hi = x.astype(BF16)
    return hi, (x - hi.astype(F32)).astype(BF16)


def split_three(x):
    first = x.astype(BF16)
    rest = x - first.astype(F32)
    second = rest.astype(BF16)
    return first, second, (rest - second.astype(F32)).astype(BF16)


def beside(*blocks):
    return jnp.concatenate(blocks, axis=1)


def above(*blocks):
    return jnp.concatenate(blocks, axis=0)


def gram_weights(gram):
    first, second, third = split_three(gram)
    return above(beside(first, third), beside(second, jnp.zeros_like(second)))


def inverse_of(x):
    guess = pl.reciprocal(x, approx=True)
    return guess * (2.0 - x * guess)


def eliminate(grown, inner):
    tiles = grown.shape[0] // 8
    width = grown.shape[1]
    x = [grown[8 * t:8 * t + 8] for t in range(tiles)]
    a = [inner[8 * t:8 * t + 8] for t in range(tiles)]
    row_id = lax.broadcasted_iota(jnp.int32, (8, width), 0)
    for t in range(tiles):
        column = {}
        for j in range(8):
            for s in range(t, tiles):
                column[j, s] = jnp.broadcast_to(a[s][:, 8 * t + j:8 * t + j + 1], (8, width))
        pivots = jnp.ones((8, width), F32)
        for j in range(8):
            inverse = inverse_of(jnp.broadcast_to(column[j, t][j:j + 1], (8, width)))
            pivots = jnp.where(row_id == j, column[j, t], pivots)
            factor = {s: column[j, s] * inverse for s in range(t, tiles)}
            factor[t] = jnp.where(row_id > j, factor[t], 0.0)
            later = {i: jnp.broadcast_to(column[i, t][j:j + 1], (8, width)) for i in range(j + 1, 8)}
            x_row = jnp.broadcast_to(x[t][j:j + 1], (8, width))
            a_row = jnp.broadcast_to(a[t][j:j + 1], a[t].shape)
            for s in range(t, tiles):
                for i in range(j + 1, 8):
                    column[i, s] = column[i, s] - factor[s] * later[i]
                x[s] = x[s] - factor[s] * x_row
                if s > t:
                    a[s] = a[s] - factor[s][:, :a_row.shape[1]] * a_row
            if t < tiles - 1:
                a[t] = a[t] - factor[t][:, :a_row.shape[1]] * a_row
        x[t] = x[t] * lax.rsqrt(pivots)
    return above(*x)


def refine_step(weights, basis_t):
    rank, periods = basis_t.shape
    b1, b2, b3 = split_three(basis_t)
    zero = jnp.zeros_like(b1)
    product = jnp.dot(above(beside(b1, b1), beside(b2, b2), beside(b3, zero)), weights,
                      preferred_element_type=F32)
    low, high = product[:, :periods], product[:, periods:]
    grown = low[:rank] + ((low[rank:2 * rank] + high[:rank]) + (low[2 * rank:] + high[rank:2 * rank]))
    g1, g2, g3 = split_three(grown)
    product = lax.dot_general(
        above(beside(g1, g1, g1), beside(g2, g2, zero), beside(g3, zero, zero)),
        beside(g1, g2, g3), (((1,), (1,)), ((), ())), preferred_element_type=F32)
    inner = product[:rank] + (product[rank:2 * rank] + product[2 * rank:])
    return eliminate(grown, inner)


def outer_of(basis_t):
    q1, q2, q3 = split_three(basis_t)
    return lax.dot_general(above(q1, q1, q1, q2, q2, q3), above(q1, q2, q3, q1, q2, q1),
                           (((0,), (0,)), ((), ())), preferred_element_type=F32)


def kernel(cells, total_rows, field, gain_any, start_any, out, buf, parts, out_buf, gain_ref, start_ref, gram_part,
           scattered, slots, gram_full, proj_ref, local_sem, small_sem, out_sem, send1, recv1, send2, recv2,
           relay_send, relay_recv, rs_send, rs_recv, bc_send, bc_recv, ag_send, ag_recv):
    me = lax.axis_index("per")
    my_cell = lax.axis_index("cells")
    sib = me + 1 - 2 * lax.rem(me, 2)
    peer = lax.rem(me + 2, 4)
    cross = lax.rem(sib + 2, 4)
    base = 2 * (1 - me // 2)
    others = (sib, peer, cross)
    own = field.shape[0]
    layers = field.shape[2]
    rows = 2 * layers

    def lanes(j):
        return pl.ds(pl.multiple_of(j * 128, 128), 128)

    local = []
    for index, j in enumerate((me,) + others):
        copy = pltpu.make_async_copy(field.at[:, :, :, lanes(j)], buf.at[j, me], local_sem.at[index])
        copy.start()
        local.append(copy)

    small = [pltpu.make_async_copy(gain_any, gain_ref, small_sem.at[0]),
             pltpu.make_async_copy(start_any, start_ref, small_sem.at[1])]
    for copy in small:
        copy.start()

    barrier = pltpu.get_barrier_semaphore()
    for other in others:
        pl.semaphore_signal(barrier, inc=1, device_id={"per": other}, device_id_type=MESH)

    def greet(step, carry):
        pl.semaphore_signal(barrier, inc=1, device_id={"cells": lax.rem(my_cell + step, cells)},
                            device_id_type=MESH)
        return carry

    lax.fori_loop(1, cells, greet, 0)
    pl.semaphore_wait(barrier, 3 + cells - 1)

    def remote(src, dst, send, recv, other):
        return pltpu.make_async_remote_copy(src_ref=src, dst_ref=dst, send_sem=send, recv_sem=recv,
                                            device_id={"per": other}, device_id_type=MESH)

    first = {}
    for a in range(2):
        for rel in (1, 2, 0):
            other = others[rel]
            copy = remote(field.at[:, a, :, lanes(other)], buf.at[other, me, :, a],
                          send1.at[rel, a], recv1.at[rel, a], other)
            copy.start()
            first[rel, a] = copy

    second = []
    for index, j in enumerate((me, peer, cross)):
        copy = remote(field.at[:, :, :, lanes(j)], buf.at[j, me], send2.at[index], recv2.at[index], sib)
        copy.start()
        second.append(copy)

    for copy in small:
        copy.wait()
    gain_row = gain_ref[...]
    gain_col = jnp.broadcast_to(gain_row, (128, 128)).T
    basis_t = start_ref[...]

    acc = jnp.zeros((256, 256), F32)
    for copy in local:
        copy.wait()
    mine = buf.at[me].reshape(128 * rows, 128)
    for a in range(2):
        for rel in range(3):
            first[rel, a].wait_recv()
        for pair in range(layers // 2):
            block = []
            for l in (2 * pair, 2 * pair + 1):
                x = mine[pl.ds(a * layers + l, 128, stride=rows), :]
                hi, lo = split_two(x)
                y = jnp.concatenate([hi, lo], axis=0)
                parts[me, a * layers + l] = y
                block.append(y)
            both = jnp.concatenate(block, axis=1)
            acc = acc + lax.dot_general(both, both, (((1,), (1,)), ((), ())),
                                        preferred_element_type=F32)
    gram_part[...] = (acc[:128, :128] + acc[128:, 128:]) + (acc[:128, 128:] + acc[128:, :128])

    def own_rows(g):
        return pl.ds(pl.multiple_of(g * own, own), own)

    scatter = []
    for rel in (1, 2, 0):
        copy = remote(gram_part.at[own_rows(others[rel])], scattered.at[rel], rs_send.at[rel],
                      rs_recv.at[rel], others[rel])
        copy.start()
        scatter.append(copy)
    relay_a = remote(buf.at[me, pl.ds(base, 2)], buf.at[me, pl.ds(base, 2)], relay_send.at[0],
                     relay_recv.at[0], sib)
    relay_a.start()
    for copy in scatter:
        copy.wait_recv()
    slots[my_cell] = (gram_part[own_rows(me), :] + scattered[0]) + (scattered[1] + scattered[2])

    def broadcast(step):
        other = lax.rem(my_cell + step, cells)
        return pltpu.make_async_remote_copy(
            src_ref=slots.at[my_cell], dst_ref=slots.at[my_cell], send_sem=bc_send.at[other],
            recv_sem=bc_recv.at[my_cell], device_id={"cells": other}, device_id_type=MESH)

    def arrival(step):
        other = lax.rem(my_cell + step, cells)
        return pltpu.make_async_remote_copy(
            src_ref=slots.at[other], dst_ref=slots.at[other], send_sem=bc_send.at[other],
            recv_sem=bc_recv.at[other], device_id={"cells": other}, device_id_type=MESH)

    def start_broadcast(step, carry):
        broadcast(step).start()
        return carry

    def wait_broadcast(step, carry):
        arrival(step).wait_recv()
        return carry

    def wait_sent(step, carry):
        broadcast(step).wait_send()
        return carry

    lax.fori_loop(1, cells, start_broadcast, 0)

    across = []
    for rel, j in ((1, me), (2, sib)):
        copy = remote(field.at[:, :, :, lanes(j)], buf.at[j, me], send2.at[2 + rel], recv2.at[2 + rel],
                      others[rel])
        copy.start()
        across.append(copy)

    def prepare(j, g):
        source = buf.at[j, g].reshape(own * rows, 128)
        for r in range(rows):
            hi, lo = split_two(source[pl.ds(r, own, stride=rows), :])
            parts[j, r, own_rows(g), :] = hi
            parts[j, r, pl.ds(pl.multiple_of(128 + g * own, own), own), :] = lo

    for j in (sib, peer, cross):
        prepare(j, me)
    for copy in second:
        copy.wait_recv()
    for j in (sib, peer, cross):
        prepare(j, sib)

    lax.fori_loop(1, cells, wait_broadcast, 0)

    def add(step, total):
        return total + slots[step]

    gram_full[own_rows(me), :] = lax.fori_loop(1, cells, add, slots[0])
    gather = []
    for rel in (1, 2, 0):
        copy = remote(gram_full.at[own_rows(me)], gram_full.at[own_rows(me)], ag_send.at[rel],
                      ag_recv.at[rel], others[rel])
        copy.start()
        gather.append(copy)
    for copy in gather:
        copy.wait_recv()

    weights = gram_weights(gram_full[...] * gain_row * gain_col * (1.0 / total_rows))
    basis_t = refine_step(weights, basis_t)
    relay_a.wait_recv()
    for g in (peer, cross):
        prepare(sib, g)
    for step in range(1, ITERS - 1):
        basis_t = refine_step(weights, basis_t)
    for copy in across:
        copy.wait_recv()
    relay_b = remote(buf.at[peer, pl.ds(base, 2)], buf.at[peer, pl.ds(base, 2)], relay_send.at[1],
                     relay_recv.at[1], sib)
    relay_b.start()
    for g in (peer, cross):
        prepare(peer, g)
    basis_t = refine_step(weights, basis_t)
    proj_ref[...] = outer_of(basis_t)
    hi, lo = split_two(proj_ref[own_rows(me), :] * gain_row)
    weights = above(beside(hi, hi), beside(lo, jnp.zeros_like(lo)))

    written = []
    for index, j in enumerate((me,) + others):
        if index == 3:
            relay_b.wait_recv()
            for g in (peer, cross):
                prepare(cross, g)
        target = out_buf.at[j].reshape(own * rows, 128)
        for r in range(0, rows, 2):
            result = jnp.dot(weights, beside(parts[j, r], parts[j, r + 1]), preferred_element_type=F32)
            result = result[:own] + result[own:]
            target[pl.ds(r, own, stride=rows), :] = result[:, :128]
            target[pl.ds(r + 1, own, stride=rows), :] = result[:, 128:]
        copy = pltpu.make_async_copy(out_buf.at[j], out.at[j], out_sem.at[index])
        copy.start()
        written.append(copy)

    for copy in list(first.values()) + second + across + scatter + gather + [relay_a, relay_b]:
        copy.wait_send()
    lax.fori_loop(1, cells, wait_sent, 0)
    for copy in written:
        copy.wait()


def per_device(field, period_gain, start_basis):
    cells = lax.axis_size("cells")
    own, _, layers, width = field.shape
    total_rows = 2.0 * layers * width * cells
    any_space = pl.BlockSpec(memory_space=pl.ANY)
    dma = pltpu.SemaphoreType.DMA
    result = pl.pallas_call(
        functools.partial(kernel, cells, total_rows),
        out_shape=jax.ShapeDtypeStruct((4, own, 2, layers, 128), F32),
        in_specs=[any_space, any_space, any_space],
        out_specs=any_space,
        scratch_shapes=[
            pltpu.VMEM((4, 4, own, 2, layers, 128), F32),
            pltpu.VMEM((4, 2 * layers, 256, 128), BF16),
            pltpu.VMEM((4, own, 2, layers, 128), F32),
            pltpu.VMEM((1, 128), F32),
            pltpu.VMEM(start_basis.shape[::-1], F32),
            pltpu.VMEM((128, 128), F32),
            pltpu.VMEM((3, own, 128), F32),
            pltpu.VMEM((cells, own, 128), F32),
            pltpu.VMEM((128, 128), F32),
            pltpu.VMEM((128, 128), F32),
            dma((4,)), dma((2,)), dma((4,)),
            dma((3, 2)), dma((3, 2)),
            dma((5,)), dma((5,)),
            dma((2,)), dma((2,)),
            dma((3,)), dma((3,)),
            dma((cells,)), dma((cells,)),
            dma((3,)), dma((3,)),
        ],
        compiler_params=pltpu.CompilerParams(
            collective_id=0, has_side_effects=True, vmem_limit_bytes=56 * 1024 * 1024),
        name="factor_and_project",
    )(field, period_gain.reshape(1, -1), start_basis.T)
    return result.transpose(1, 2, 3, 0, 4).reshape(field.shape)


def solution(mesh):
    in_specs = (P("per", None, None, "cells"), P(), P())
    out_specs = P("per", None, None, "cells")
    return jax.shard_map(
        per_device, mesh=mesh, in_specs=in_specs, out_specs=out_specs, check_vma=False
    )
```

```python
import functools
import jax
import jax.numpy as jnp
from jax import lax
from jax.experimental import pallas as pl
from jax.experimental.pallas import tpu as pltpu
from jax.sharding import PartitionSpec as P

ITERS = 3
HIGH = lax.Precision.HIGHEST
MESH = pl.DeviceIdType.MESH
F32 = jnp.float32
BF16 = jnp.bfloat16


def split_two(x):
    hi = x.astype(BF16)
    return hi, (x - hi.astype(F32)).astype(BF16)


def split_three(x):
    first = x.astype(BF16)
    rest = x - first.astype(F32)
    second = rest.astype(BF16)
    return first, second, (rest - second.astype(F32)).astype(BF16)


def beside(*blocks):
    return jnp.concatenate(blocks, axis=1)


def above(*blocks):
    return jnp.concatenate(blocks, axis=0)


def gram_weights(gram):
    first, second, third = split_three(gram)
    return above(beside(first, third), beside(second, jnp.zeros_like(second)))


def inverse_of(x):
    guess = pl.reciprocal(x, approx=True)
    return guess * (2.0 - x * guess)


def eliminate(grown, inner):
    tiles = grown.shape[0] // 8
    width = grown.shape[1]
    x = [grown[8 * t:8 * t + 8] for t in range(tiles)]
    a = [inner[8 * t:8 * t + 8] for t in range(tiles)]
    row_id = lax.broadcasted_iota(jnp.int32, (8, width), 0)
    for t in range(tiles):
        column = {}
        for j in range(8):
            for s in range(t, tiles):
                column[j, s] = jnp.broadcast_to(a[s][:, 8 * t + j:8 * t + j + 1], (8, width))
        pivots = jnp.ones((8, width), F32)
        for j in range(8):
            inverse = inverse_of(jnp.broadcast_to(column[j, t][j:j + 1], (8, width)))
            pivots = jnp.where(row_id == j, column[j, t], pivots)
            factor = {s: column[j, s] * inverse for s in range(t, tiles)}
            factor[t] = jnp.where(row_id > j, factor[t], 0.0)
            later = {i: jnp.broadcast_to(column[i, t][j:j + 1], (8, width)) for i in range(j + 1, 8)}
            x_row = jnp.broadcast_to(x[t][j:j + 1], (8, width))
            a_row = jnp.broadcast_to(a[t][j:j + 1], a[t].shape)
            for s in range(t, tiles):
                for i in range(j + 1, 8):
                    column[i, s] = column[i, s] - factor[s] * later[i]
                x[s] = x[s] - factor[s] * x_row
                if s > t:
                    a[s] = a[s] - factor[s][:, :a_row.shape[1]] * a_row
            if t < tiles - 1:
                a[t] = a[t] - factor[t][:, :a_row.shape[1]] * a_row
        x[t] = x[t] * lax.rsqrt(pivots)
    return above(*x)


def refine_step(weights, basis_t):
    rank, periods = basis_t.shape
    b1, b2, b3 = split_three(basis_t)
    zero = jnp.zeros_like(b1)
    product = jnp.dot(above(beside(b1, b1), beside(b2, b2), beside(b3, zero)), weights,
                      preferred_element_type=F32)
    low, high = product[:, :periods], product[:, periods:]
    grown = low[:rank] + ((low[rank:2 * rank] + high[:rank]) + (low[2 * rank:] + high[rank:2 * rank]))
    g1, g2, g3 = split_three(grown)
    product = lax.dot_general(
        above(beside(g1, g1, g1), beside(g2, g2, zero), beside(g3, zero, zero)),
        beside(g1, g2, g3), (((1,), (1,)), ((), ())), preferred_element_type=F32)
    inner = product[:rank] + (product[rank:2 * rank] + product[2 * rank:])
    return eliminate(grown, inner)


def outer_of(basis_t):
    q1, q2, q3 = split_three(basis_t)
    return lax.dot_general(above(q1, q1, q1, q2, q2, q3), above(q1, q2, q3, q1, q2, q1),
                           (((0,), (0,)), ((), ())), preferred_element_type=F32)


def kernel(cells, total_rows, field, gain_any, start_any, out, buf, parts, out_buf, gain_ref, start_ref, gram_part,
           scattered, slots, gram_full, proj_ref, local_sem, small_sem, out_sem, send1, recv1, send2, recv2, send3, recv3,
           relay_send, relay_recv, rs_send, rs_recv, bc_send, bc_recv, ag_send, ag_recv):
    me = lax.axis_index("per")
    my_cell = lax.axis_index("cells")
    sib = me + 1 - 2 * lax.rem(me, 2)
    peer = lax.rem(me + 2, 4)
    cross = lax.rem(sib + 2, 4)
    base = 2 * (1 - me // 2)
    others = (sib, peer, cross)
    own = field.shape[0]
    layers = field.shape[2]
    rows = 2 * layers

    def lanes(j):
        return pl.ds(pl.multiple_of(j * 128, 128), 128)

    local = []
    for index, j in enumerate((me,) + others):
        copy = pltpu.make_async_copy(field.at[:, :, :, lanes(j)], buf.at[j, me], local_sem.at[index])
        copy.start()
        local.append(copy)

    small = [pltpu.make_async_copy(gain_any, gain_ref, small_sem.at[0]),
             pltpu.make_async_copy(start_any, start_ref, small_sem.at[1])]
    for copy in small:
        copy.start()

    barrier = pltpu.get_barrier_semaphore()
    parity = lax.rem(my_cell, 2)
    half = my_cell // 2
    halves = cells // 2
    pair_cell = my_cell + 1 - 2 * parity
    group = [(g, c) for c in (my_cell, pair_cell) for g in (me,) + others]
    for g, c in group[1:]:
        pl.semaphore_signal(barrier, inc=1, device_id={"per": g, "cells": c}, device_id_type=MESH)

    def distant(step):
        return lax.rem(half + step, halves)

    def greet(step, carry):
        pl.semaphore_signal(barrier, inc=1, device_id={"cells": 2 * distant(step) + parity},
                            device_id_type=MESH)
        return carry

    lax.fori_loop(1, halves, greet, 0)
    pl.semaphore_wait(barrier, 7 + halves - 1)

    def remote(src, dst, send, recv, other):
        return pltpu.make_async_remote_copy(src_ref=src, dst_ref=dst, send_sem=send, recv_sem=recv,
                                            device_id={"per": other}, device_id_type=MESH)

    first = {}
    for a in range(2):
        for rel in (1, 2, 0):
            other = others[rel]
            copy = remote(field.at[:, a, :, lanes(other)], buf.at[other, me, :, a],
                          send1.at[rel, a], recv1.at[rel, a], other)
            copy.start()
            first[rel, a] = copy

    second = []
    for index, j in enumerate((me, peer, cross)):
        copy = remote(field.at[:, :, :, lanes(j)], buf.at[j, me], send2.at[index], recv2.at[index], sib)
        copy.start()
        second.append(copy)

    for copy in small:
        copy.wait()
    gain_row = gain_ref[...]
    gain_col = jnp.broadcast_to(gain_row, (128, 128)).T
    basis_t = start_ref[...]

    acc = jnp.zeros((256, 256), F32)
    for copy in local:
        copy.wait()
    mine = buf.at[me].reshape(128 * rows, 128)
    for a in range(2):
        for rel in range(3):
            first[rel, a].wait_recv()
        for pair in range(layers // 2):
            block = []
            for l in (2 * pair, 2 * pair + 1):
                x = mine[pl.ds(a * layers + l, 128, stride=rows), :]
                hi, lo = split_two(x)
                y = jnp.concatenate([hi, lo], axis=0)
                parts[me, a * layers + l] = y
                block.append(y)
            both = jnp.concatenate(block, axis=1)
            acc = acc + lax.dot_general(both, both, (((1,), (1,)), ((), ())),
                                        preferred_element_type=F32)
    gram_part[...] = (acc[:128, :128] + acc[128:, 128:]) + (acc[:128, 128:] + acc[128:, :128])

    def own_rows(g):
        return pl.ds(pl.multiple_of(g * own, own), own)

    def share(g, c):
        return pl.ds(pl.multiple_of((lax.rem(c, 2) * 4 + g) * (own // 2), own // 2), own // 2)

    def to_group(src, dst, send, recv, g, c):
        return pltpu.make_async_remote_copy(src_ref=src, dst_ref=dst, send_sem=send, recv_sem=recv,
                                            device_id={"per": g, "cells": c}, device_id_type=MESH)

    order = (6, 7, 5, 4, 2, 3, 1)
    mine_only = share(me, my_cell)

    scatter = []
    for rel in order:
        g, c = group[rel]
        copy = to_group(gram_part.at[share(g, c)], scattered.at[rel], rs_send.at[rel],
                        rs_recv.at[rel], g, c)
        copy.start()
        scatter.append(copy)
    relay_a = remote(buf.at[me, pl.ds(base, 2)], buf.at[me, pl.ds(base, 2)], relay_send.at[0],
                     relay_recv.at[0], sib)
    relay_a.start()
    for copy in scatter:
        copy.wait_recv()
    slots[half] = ((gram_part[mine_only, :] + scattered[1]) + (scattered[2] + scattered[3])) + (
        (scattered[4] + scattered[5]) + (scattered[6] + scattered[7]))

    def broadcast(step):
        other = distant(step)
        return pltpu.make_async_remote_copy(
            src_ref=slots.at[half], dst_ref=slots.at[half], send_sem=bc_send.at[other],
            recv_sem=bc_recv.at[half], device_id={"cells": 2 * other + parity}, device_id_type=MESH)

    def arrival(step):
        other = distant(step)
        return pltpu.make_async_remote_copy(
            src_ref=slots.at[other], dst_ref=slots.at[other], send_sem=bc_send.at[other],
            recv_sem=bc_recv.at[other], device_id={"cells": 2 * other + parity}, device_id_type=MESH)

    def start_broadcast(step, carry):
        broadcast(step).start()
        return carry

    def wait_broadcast(step, carry):
        arrival(step).wait_recv()
        return carry

    def wait_sent(step, carry):
        broadcast(step).wait_send()
        return carry

    lax.fori_loop(1, halves, start_broadcast, 0)

    across = {}
    for a in range(2):
        for rel, j in ((1, me), (2, sib)):
            across[rel, a] = remote(field.at[:, a, :, lanes(j)], buf.at[j, me, :, a],
                                    send3.at[rel - 1, a], recv3.at[rel - 1, a], others[rel])

    def start_across(a):
        for rel in (1, 2):
            across[rel, a].start()

    def relay_across(a):
        for rel in (1, 2):
            across[rel, a].wait_recv()
        place = buf.at[peer, pl.ds(base, 2), :, a]
        copy = remote(place, place, relay_send.at[1 + a], relay_recv.at[1 + a], sib)
        copy.start()
        return copy

    start_across(0)

    def prepare(j, g):
        source = buf.at[j, g].reshape(own * rows, 128)
        for r in range(rows):
            hi, lo = split_two(source[pl.ds(r, own, stride=rows), :])
            parts[j, r, own_rows(g), :] = hi
            parts[j, r, pl.ds(pl.multiple_of(128 + g * own, own), own), :] = lo

    for j in (sib, peer, cross):
        prepare(j, me)
    for copy in second:
        copy.wait_recv()
    for j in (sib, peer, cross):
        prepare(j, sib)

    lax.fori_loop(1, halves, wait_broadcast, 0)

    def add(step, total):
        return total + slots[step]

    gram_full[mine_only, :] = lax.fori_loop(1, halves, add, slots[0])
    gather = []
    for rel in order:
        g, c = group[rel]
        copy = to_group(gram_full.at[mine_only], gram_full.at[mine_only], ag_send.at[rel],
                        ag_recv.at[rel], g, c)
        copy.start()
        gather.append(copy)
    for copy in gather:
        copy.wait_recv()

    start_across(1)
    weights = gram_weights(gram_full[...] * gain_row * gain_col * (1.0 / total_rows))
    basis_t = refine_step(weights, basis_t)
    relay_a.wait_recv()
    for g in (peer, cross):
        prepare(sib, g)
    relays = [relay_across(0)]
    for step in range(1, ITERS):
        basis_t = refine_step(weights, basis_t)
    relays.append(relay_across(1))
    proj_ref[...] = outer_of(basis_t)
    hi, lo = split_two(proj_ref[own_rows(me), :] * gain_row)
    weights = above(beside(hi, hi), beside(lo, jnp.zeros_like(lo)))

    for g in (peer, cross):
        prepare(peer, g)
    written = []
    for index, j in enumerate((me,) + others):
        if index == 3:
            for copy in relays:
                copy.wait_recv()
            for g in (peer, cross):
                prepare(cross, g)
        target = out_buf.at[j].reshape(own * rows, 128)
        for r in range(0, rows, 2):
            result = jnp.dot(weights, beside(parts[j, r], parts[j, r + 1]), preferred_element_type=F32)
            result = result[:own] + result[own:]
            target[pl.ds(r, own, stride=rows), :] = result[:, :128]
            target[pl.ds(r + 1, own, stride=rows), :] = result[:, 128:]
        copy = pltpu.make_async_copy(out_buf.at[j], out.at[:, :, :, lanes(j)], out_sem.at[index])
        copy.start()
        written.append(copy)

    for copy in list(first.values()) + second + list(across.values()) + scatter + gather + [relay_a] + relays:
        copy.wait_send()
    lax.fori_loop(1, halves, wait_sent, 0)
    for copy in written:
        copy.wait()


def per_device(field, period_gain, start_basis):
    cells = lax.axis_size("cells")
    own, _, layers, width = field.shape
    total_rows = 2.0 * layers * width * cells
    any_space = pl.BlockSpec(memory_space=pl.ANY)
    dma = pltpu.SemaphoreType.DMA
    return pl.pallas_call(
        functools.partial(kernel, cells, total_rows),
        out_shape=jax.ShapeDtypeStruct(field.shape, F32),
        in_specs=[any_space, any_space, any_space],
        out_specs=any_space,
        scratch_shapes=[
            pltpu.VMEM((4, 4, own, 2, layers, 128), F32),
            pltpu.VMEM((4, 2 * layers, 256, 128), BF16),
            pltpu.VMEM((4, own, 2, layers, 128), F32),
            pltpu.VMEM((1, 128), F32),
            pltpu.VMEM(start_basis.shape[::-1], F32),
            pltpu.VMEM((128, 128), F32),
            pltpu.VMEM((8, own // 2, 128), F32),
            pltpu.VMEM((cells // 2, own // 2, 128), F32),
            pltpu.VMEM((128, 128), F32),
            pltpu.VMEM((128, 128), F32),
            dma((4,)), dma((2,)), dma((4,)),
            dma((3, 2)), dma((3, 2)),
            dma((3,)), dma((3,)),
            dma((2, 2)), dma((2, 2)),
            dma((3,)), dma((3,)),
            dma((8,)), dma((8,)),
            dma((cells // 2,)), dma((cells // 2,)),
            dma((8,)), dma((8,)),
        ],
        compiler_params=pltpu.CompilerParams(
            collective_id=0, has_side_effects=True, vmem_limit_bytes=56 * 1024 * 1024),
        name="factor_and_project",
    )(field, period_gain.reshape(1, -1), start_basis.T)


def solution(mesh):
    in_specs = (P("per", None, None, "cells"), P(), P())
    out_specs = P("per", None, None, "cells")
    return jax.shard_map(
        per_device, mesh=mesh, in_specs=in_specs, out_specs=out_specs, check_vma=False
    )
```

```python
import functools
import jax
import jax.numpy as jnp
from jax import lax
from jax.experimental import pallas as pl
from jax.experimental.pallas import tpu as pltpu
from jax.sharding import PartitionSpec as P

ITERS = 3
HIGH = lax.Precision.HIGHEST
MESH = pl.DeviceIdType.MESH
F32 = jnp.float32
BF16 = jnp.bfloat16


def split_two(x):
    hi = x.astype(BF16)
    return hi, (x - hi.astype(F32)).astype(BF16)


def split_three(x):
    first = x.astype(BF16)
    rest = x - first.astype(F32)
    second = rest.astype(BF16)
    return first, second, (rest - second.astype(F32)).astype(BF16)


def beside(*blocks):
    return jnp.concatenate(blocks, axis=1)


def above(*blocks):
    return jnp.concatenate(blocks, axis=0)


def gram_weights(gram):
    first, second, third = split_three(gram)
    return above(beside(first, third), beside(second, jnp.zeros_like(second)))


def inverse_of(x):
    guess = pl.reciprocal(x, approx=True)
    return guess * (2.0 - x * guess)


def eliminate(grown, inner):
    tiles = grown.shape[0] // 8
    width = grown.shape[1]
    x = [grown[8 * t:8 * t + 8] for t in range(tiles)]
    a = [inner[8 * t:8 * t + 8] for t in range(tiles)]
    row_id = lax.broadcasted_iota(jnp.int32, (8, width), 0)
    for t in range(tiles):
        column = {}
        for j in range(8):
            for s in range(t, tiles):
                column[j, s] = jnp.broadcast_to(a[s][:, 8 * t + j:8 * t + j + 1], (8, width))
        pivots = jnp.ones((8, width), F32)
        for j in range(8):
            inverse = inverse_of(jnp.broadcast_to(column[j, t][j:j + 1], (8, width)))
            pivots = jnp.where(row_id == j, column[j, t], pivots)
            factor = {s: column[j, s] * inverse for s in range(t, tiles)}
            factor[t] = jnp.where(row_id > j, factor[t], 0.0)
            later = {i: jnp.broadcast_to(column[i, t][j:j + 1], (8, width)) for i in range(j + 1, 8)}
            x_row = jnp.broadcast_to(x[t][j:j + 1], (8, width))
            a_row = jnp.broadcast_to(a[t][j:j + 1], a[t].shape)
            for s in range(t, tiles):
                for i in range(j + 1, 8):
                    column[i, s] = column[i, s] - factor[s] * later[i]
                x[s] = x[s] - factor[s] * x_row
                if s > t:
                    a[s] = a[s] - factor[s][:, :a_row.shape[1]] * a_row
            if t < tiles - 1:
                a[t] = a[t] - factor[t][:, :a_row.shape[1]] * a_row
        x[t] = x[t] * lax.rsqrt(pivots)
    return above(*x)


def refine_step(weights, basis_t):
    rank, periods = basis_t.shape
    b1, b2, b3 = split_three(basis_t)
    zero = jnp.zeros_like(b1)
    product = jnp.dot(above(beside(b1, b1), beside(b2, b2), beside(b3, zero)), weights,
                      preferred_element_type=F32)
    low, high = product[:, :periods], product[:, periods:]
    grown = low[:rank] + ((low[rank:2 * rank] + high[:rank]) + (low[2 * rank:] + high[rank:2 * rank]))
    g1, g2, g3 = split_three(grown)
    product = lax.dot_general(
        above(beside(g1, g1, g1), beside(g2, g2, zero), beside(g3, zero, zero)),
        beside(g1, g2, g3), (((1,), (1,)), ((), ())), preferred_element_type=F32)
    inner = product[:rank] + (product[rank:2 * rank] + product[2 * rank:])
    return eliminate(grown, inner)


def outer_of(basis_t):
    q1, q2, q3 = split_three(basis_t)
    return lax.dot_general(above(q1, q1, q1, q2, q2, q3), above(q1, q2, q3, q1, q2, q1),
                           (((0,), (0,)), ((), ())), preferred_element_type=F32)


def kernel(cells, total_rows, field, gain_any, start_any, buf, weights_ref, mine, gain_ref, start_ref, gram_part,
           scattered, slots, gram_full, proj_ref, local_sem, small_sem, back_sem, send1, recv1, send2, recv2, send3, recv3,
           relay_send, relay_recv, rs_send, rs_recv, bc_send, bc_recv, ag_send, ag_recv):
    me = lax.axis_index("per")
    my_cell = lax.axis_index("cells")
    sib = me + 1 - 2 * lax.rem(me, 2)
    peer = lax.rem(me + 2, 4)
    cross = lax.rem(sib + 2, 4)
    base = 2 * (1 - me // 2)
    others = (sib, peer, cross)
    own = field.shape[0]
    layers = field.shape[2]
    rows = 2 * layers

    def lanes(j):
        return pl.ds(pl.multiple_of(j * 128, 128), 128)

    local = []
    for index, j in enumerate((me,) + others):
        target = mine.at[me] if index == 0 else buf.at[j, me]
        copy = pltpu.make_async_copy(field.at[:, :, :, lanes(j)], target, local_sem.at[index])
        copy.start()
        local.append(copy)

    small = [pltpu.make_async_copy(gain_any, gain_ref, small_sem.at[0]),
             pltpu.make_async_copy(start_any, start_ref, small_sem.at[1])]
    for copy in small:
        copy.start()

    barrier = pltpu.get_barrier_semaphore()
    parity = lax.rem(my_cell, 2)
    half = my_cell // 2
    halves = cells // 2
    pair_cell = my_cell + 1 - 2 * parity
    group = [(g, c) for c in (my_cell, pair_cell) for g in (me,) + others]
    for g, c in group[1:]:
        pl.semaphore_signal(barrier, inc=1, device_id={"per": g, "cells": c}, device_id_type=MESH)

    def distant(step):
        return lax.rem(half + step, halves)

    def greet(step, carry):
        pl.semaphore_signal(barrier, inc=1, device_id={"cells": 2 * distant(step) + parity},
                            device_id_type=MESH)
        return carry

    lax.fori_loop(1, halves, greet, 0)
    pl.semaphore_wait(barrier, 7 + halves - 1)

    def remote(src, dst, send, recv, other):
        return pltpu.make_async_remote_copy(src_ref=src, dst_ref=dst, send_sem=send, recv_sem=recv,
                                            device_id={"per": other}, device_id_type=MESH)

    first = {}
    for a in range(2):
        for rel in (1, 2, 0):
            other = others[rel]
            copy = remote(field.at[:, a, :, lanes(other)], mine.at[me, :, a],
                          send1.at[rel, a], recv1.at[rel, a], other)
            copy.start()
            first[rel, a] = copy

    second = []
    for index, j in enumerate((me, peer, cross)):
        copy = remote(field.at[:, :, :, lanes(j)], buf.at[j, me], send2.at[index], recv2.at[index], sib)
        copy.start()
        second.append(copy)

    for copy in small:
        copy.wait()
    gain_row = gain_ref[...]
    gain_col = jnp.broadcast_to(gain_row, (128, 128)).T
    basis_t = start_ref[...]

    acc = jnp.zeros((256, 256), F32)
    local[0].wait()
    flat = mine.reshape(128 * rows, 128)
    for a in range(2):
        for rel in range(3):
            first[rel, a].wait_recv()
        for pair in range(layers // 2):
            block = []
            for l in (2 * pair, 2 * pair + 1):
                block.append(above(*split_two(flat[pl.ds(a * layers + l, 128, stride=rows), :])))
            both = beside(*block)
            acc = acc + lax.dot_general(both, both, (((1,), (1,)), ((), ())),
                                        preferred_element_type=F32)
    gram_part[...] = (acc[:128, :128] + acc[128:, 128:]) + (acc[:128, 128:] + acc[128:, :128])

    def own_rows(g):
        return pl.ds(pl.multiple_of(g * own, own), own)

    def share(g, c):
        return pl.ds(pl.multiple_of((lax.rem(c, 2) * 4 + g) * (own // 2), own // 2), own // 2)

    def to_group(src, dst, send, recv, g, c):
        return pltpu.make_async_remote_copy(src_ref=src, dst_ref=dst, send_sem=send, recv_sem=recv,
                                            device_id={"per": g, "cells": c}, device_id_type=MESH)

    order = (6, 7, 5, 4, 2, 3, 1)
    mine_only = share(me, my_cell)

    scatter = []
    for rel in order:
        g, c = group[rel]
        copy = to_group(gram_part.at[share(g, c)], scattered.at[rel], rs_send.at[rel],
                        rs_recv.at[rel], g, c)
        copy.start()
        scatter.append(copy)
    back = pltpu.make_async_copy(mine, buf.at[me], back_sem.at[0])
    back.start()
    relay_a = remote(mine.at[pl.ds(base, 2)], buf.at[me, pl.ds(base, 2)], relay_send.at[0],
                     relay_recv.at[0], sib)
    relay_a.start()
    for copy in scatter:
        copy.wait_recv()
    slots[half] = ((gram_part[mine_only, :] + scattered[1]) + (scattered[2] + scattered[3])) + (
        (scattered[4] + scattered[5]) + (scattered[6] + scattered[7]))

    def broadcast(step):
        other = distant(step)
        return pltpu.make_async_remote_copy(
            src_ref=slots.at[half], dst_ref=slots.at[half], send_sem=bc_send.at[other],
            recv_sem=bc_recv.at[half], device_id={"cells": 2 * other + parity}, device_id_type=MESH)

    def arrival(step):
        other = distant(step)
        return pltpu.make_async_remote_copy(
            src_ref=slots.at[other], dst_ref=slots.at[other], send_sem=bc_send.at[other],
            recv_sem=bc_recv.at[other], device_id={"cells": 2 * other + parity}, device_id_type=MESH)

    def start_broadcast(step, carry):
        broadcast(step).start()
        return carry

    def wait_broadcast(step, carry):
        arrival(step).wait_recv()
        return carry

    def wait_sent(step, carry):
        broadcast(step).wait_send()
        return carry

    lax.fori_loop(1, halves, start_broadcast, 0)

    early = 3 * own // 8
    pieces = (pl.ds(0, early), pl.ds(early, own - early))
    across = {}
    for a in range(2):
        for rel, j in ((1, me), (2, sib)):
            across[rel, a] = remote(field.at[pieces[a], :, :, lanes(j)], buf.at[j, me, pieces[a]],
                                    send3.at[rel - 1, a], recv3.at[rel - 1, a], others[rel])

    def start_across(a):
        for rel in (1, 2):
            across[rel, a].start()

    def relay_across(a):
        for rel in (1, 2):
            across[rel, a].wait_recv()
        place = buf.at[peer, pl.ds(base, 2), pieces[a]]
        copy = remote(place, place, relay_send.at[1 + a], relay_recv.at[1 + a], sib)
        copy.start()
        return copy

    start_across(0)

    lax.fori_loop(1, halves, wait_broadcast, 0)

    def add(step, total):
        return total + slots[step]

    gram_full[mine_only, :] = lax.fori_loop(1, halves, add, slots[0])
    gather = []
    for rel in order:
        g, c = group[rel]
        copy = to_group(gram_full.at[mine_only], gram_full.at[mine_only], ag_send.at[rel],
                        ag_recv.at[rel], g, c)
        copy.start()
        gather.append(copy)
    for copy in gather:
        copy.wait_recv()

    start_across(1)
    weights = gram_weights(gram_full[...] * gain_row * gain_col * (1.0 / total_rows))
    basis_t = refine_step(weights, basis_t)
    relays = [relay_across(0)]
    for step in range(1, ITERS):
        basis_t = refine_step(weights, basis_t)
    relays.append(relay_across(1))
    proj_ref[...] = outer_of(basis_t)
    hi, lo = split_two(proj_ref[own_rows(me), :] * gain_row)
    weights_ref[...] = above(beside(hi, hi), beside(lo, jnp.zeros_like(lo)))

    for copy in second + [relay_a] + relays:
        copy.wait_recv()
    for copy in local[1:] + [back]:
        copy.wait()
    for copy in list(first.values()) + second + list(across.values()) + scatter + gather + [relay_a] + relays:
        copy.wait_send()
    lax.fori_loop(1, halves, wait_sent, 0)


def project(weights_ref, field_ref, out_ref):
    _, parts, own, _, layers, _ = field_ref.shape
    rows = 2 * layers
    source = field_ref.at[0].reshape(parts * own * rows, 128)
    target = out_ref.reshape(own * rows, 128)
    weights = weights_ref[...]
    for r in range(0, rows, 2):
        block = [above(*split_two(source[pl.ds(r + i, parts * own, stride=rows), :])) for i in range(2)]
        result = jnp.dot(weights, beside(*block), preferred_element_type=F32)
        result = result[:own] + result[own:]
        target[pl.ds(r, own, stride=rows), :] = result[:, :128]
        target[pl.ds(r + 1, own, stride=rows), :] = result[:, 128:]


def per_device(field, period_gain, start_basis):
    cells = lax.axis_size("cells")
    own, _, layers, width = field.shape
    total_rows = 2.0 * layers * width * cells
    any_space = pl.BlockSpec(memory_space=pl.ANY)
    dma = pltpu.SemaphoreType.DMA
    gathered, weights = pl.pallas_call(
        functools.partial(kernel, cells, total_rows),
        out_shape=(jax.ShapeDtypeStruct((4, 4, own, 2, layers, 128), F32),
                   jax.ShapeDtypeStruct((2 * own, 256), BF16)),
        in_specs=[any_space, any_space, any_space],
        out_specs=(any_space, pl.BlockSpec(memory_space=pltpu.VMEM)),
        scratch_shapes=[
            pltpu.VMEM((4, own, 2, layers, 128), F32),
            pltpu.VMEM((1, 128), F32),
            pltpu.VMEM(start_basis.shape[::-1], F32),
            pltpu.VMEM((128, 128), F32),
            pltpu.VMEM((8, own // 2, 128), F32),
            pltpu.VMEM((cells // 2, own // 2, 128), F32),
            pltpu.VMEM((128, 128), F32),
            pltpu.VMEM((128, 128), F32),
            dma((4,)), dma((2,)), dma((1,)),
            dma((3, 2)), dma((3, 2)),
            dma((3,)), dma((3,)),
            dma((2, 2)), dma((2, 2)),
            dma((3,)), dma((3,)),
            dma((8,)), dma((8,)),
            dma((cells // 2,)), dma((cells // 2,)),
            dma((8,)), dma((8,)),
        ],
        compiler_params=pltpu.CompilerParams(
            collective_id=0, has_side_effects=True, vmem_limit_bytes=56 * 1024 * 1024),
        name="gather_and_factor",
    )(field, period_gain.reshape(1, -1), start_basis.T)
    return pl.pallas_call(
        project,
        grid=(4,),
        out_shape=jax.ShapeDtypeStruct(field.shape, F32),
        in_specs=[pl.BlockSpec((2 * own, 256), lambda j: (0, 0)),
                  pl.BlockSpec((1, 4, own, 2, layers, 128), lambda j: (j, 0, 0, 0, 0, 0))],
        out_specs=pl.BlockSpec((own, 2, layers, 128), lambda j: (0, 0, 0, j)),
        compiler_params=pltpu.CompilerParams(vmem_limit_bytes=56 * 1024 * 1024),
        name="project",
    )(weights, gathered)


def solution(mesh):
    in_specs = (P("per", None, None, "cells"), P(), P())
    out_specs = P("per", None, None, "cells")
    return jax.shard_map(
        per_device, mesh=mesh, in_specs=in_specs, out_specs=out_specs, check_vma=False
    )
```

```python
import functools
import jax
import jax.numpy as jnp
from jax import lax
from jax.experimental import pallas as pl
from jax.experimental.pallas import tpu as pltpu
from jax.sharding import PartitionSpec as P

ITERS = 3
HIGH = lax.Precision.HIGHEST
MESH = pl.DeviceIdType.MESH
F32 = jnp.float32
BF16 = jnp.bfloat16


def split_two(x):
    hi = x.astype(BF16)
    return hi, (x - hi.astype(F32)).astype(BF16)


def split_three(x):
    first = x.astype(BF16)
    rest = x - first.astype(F32)
    second = rest.astype(BF16)
    return first, second, (rest - second.astype(F32)).astype(BF16)


def beside(*blocks):
    return jnp.concatenate(blocks, axis=1)


def above(*blocks):
    return jnp.concatenate(blocks, axis=0)


def gram_weights(gram):
    first, second, third = split_three(gram)
    return above(beside(first, third), beside(second, jnp.zeros_like(second)))


def inverse_of(x):
    guess = pl.reciprocal(x, approx=True)
    return guess * (2.0 - x * guess)


def eliminate(grown, inner):
    tiles = grown.shape[0] // 8
    width = grown.shape[1]
    x = [grown[8 * t:8 * t + 8] for t in range(tiles)]
    a = [inner[8 * t:8 * t + 8] for t in range(tiles)]
    row_id = lax.broadcasted_iota(jnp.int32, (8, width), 0)
    for t in range(tiles):
        column = {}
        for j in range(8):
            for s in range(t, tiles):
                column[j, s] = jnp.broadcast_to(a[s][:, 8 * t + j:8 * t + j + 1], (8, width))
        pivots = jnp.ones((8, width), F32)
        for j in range(8):
            inverse = inverse_of(jnp.broadcast_to(column[j, t][j:j + 1], (8, width)))
            pivots = jnp.where(row_id == j, column[j, t], pivots)
            factor = {s: column[j, s] * inverse for s in range(t, tiles)}
            factor[t] = jnp.where(row_id > j, factor[t], 0.0)
            later = {i: jnp.broadcast_to(column[i, t][j:j + 1], (8, width)) for i in range(j + 1, 8)}
            x_row = jnp.broadcast_to(x[t][j:j + 1], (8, width))
            a_row = jnp.broadcast_to(a[t][j:j + 1], a[t].shape)
            for s in range(t, tiles):
                for i in range(j + 1, 8):
                    column[i, s] = column[i, s] - factor[s] * later[i]
                x[s] = x[s] - factor[s] * x_row
                if s > t:
                    a[s] = a[s] - factor[s][:, :a_row.shape[1]] * a_row
            if t < tiles - 1:
                a[t] = a[t] - factor[t][:, :a_row.shape[1]] * a_row
        x[t] = x[t] * lax.rsqrt(pivots)
    return above(*x)


def refine_step(weights, basis_t):
    rank, periods = basis_t.shape
    b1, b2, b3 = split_three(basis_t)
    zero = jnp.zeros_like(b1)
    product = jnp.dot(above(beside(b1, b1), beside(b2, b2), beside(b3, zero)), weights,
                      preferred_element_type=F32)
    low, high = product[:, :periods], product[:, periods:]
    grown = low[:rank] + ((low[rank:2 * rank] + high[:rank]) + (low[2 * rank:] + high[rank:2 * rank]))
    g1, g2, g3 = split_three(grown)
    product = lax.dot_general(
        above(beside(g1, g1, g1), beside(g2, g2, zero), beside(g3, zero, zero)),
        beside(g1, g2, g3), (((1,), (1,)), ((), ())), preferred_element_type=F32)
    inner = product[:rank] + (product[rank:2 * rank] + product[2 * rank:])
    return eliminate(grown, inner)


def outer_of(basis_t):
    q1, q2, q3 = split_three(basis_t)
    return lax.dot_general(above(q1, q1, q1, q2, q2, q3), above(q1, q2, q3, q1, q2, q1),
                           (((0,), (0,)), ((), ())), preferred_element_type=F32)


def kernel(cells, total_rows, field, gain_any, start_any, out, buf, parts, out_buf, gain_ref, start_ref, gram_part,
           scattered, slots, gram_full, proj_ref, local_sem, small_sem, out_sem, send1, recv1, send2, recv2, send3, recv3,
           relay_send, relay_recv, rs_send, rs_recv, bc_send, bc_recv, ag_send, ag_recv):
    me = lax.axis_index("per")
    my_cell = lax.axis_index("cells")
    sib = me + 1 - 2 * lax.rem(me, 2)
    peer = lax.rem(me + 2, 4)
    cross = lax.rem(sib + 2, 4)
    base = 2 * (1 - me // 2)
    others = (sib, peer, cross)
    own = field.shape[0]
    layers = field.shape[2]
    rows = 2 * layers

    def lanes(j):
        return pl.ds(pl.multiple_of(j * 128, 128), 128)

    local = {}
    for a in range(2):
        for index, j in ((2, peer), (3, cross), (1, sib), (0, me)):
            copy = pltpu.make_async_copy(field.at[:, a, :, lanes(j)], buf.at[j, a, me],
                                         local_sem.at[index, a])
            copy.start()
            local[index, a] = copy

    small = [pltpu.make_async_copy(gain_any, gain_ref, small_sem.at[0]),
             pltpu.make_async_copy(start_any, start_ref, small_sem.at[1])]
    for copy in small:
        copy.start()

    barrier = pltpu.get_barrier_semaphore()
    parity = lax.rem(my_cell, 2)
    half = my_cell // 2
    halves = cells // 2
    pair_cell = my_cell + 1 - 2 * parity
    group = [(g, c) for c in (my_cell, pair_cell) for g in (me,) + others]
    for g, c in group[1:]:
        pl.semaphore_signal(barrier, inc=1, device_id={"per": g, "cells": c}, device_id_type=MESH)

    def distant(step):
        return lax.rem(half + step, halves)

    def greet(step, carry):
        pl.semaphore_signal(barrier, inc=1, device_id={"cells": 2 * distant(step) + parity},
                            device_id_type=MESH)
        return carry

    lax.fori_loop(1, halves, greet, 0)
    pl.semaphore_wait(barrier, 7 + halves - 1)

    def remote(src, dst, send, recv, other):
        return pltpu.make_async_remote_copy(src_ref=src, dst_ref=dst, send_sem=send, recv_sem=recv,
                                            device_id={"per": other}, device_id_type=MESH)

    first = {}
    for a in range(2):
        for rel in (1, 2, 0):
            other = others[rel]
            local[rel + 1, a].wait()
            copy = remote(buf.at[other, a, me], buf.at[other, a, me],
                          send1.at[rel, a], recv1.at[rel, a], other)
            copy.start()
            first[rel, a] = copy

    second = []
    for index, j in enumerate((me, peer, cross)):
        for a in range(2):
            if index == 0:
                local[0, a].wait()
            copy = remote(buf.at[j, a, me], buf.at[j, a, me], send2.at[index, a], recv2.at[index, a], sib)
            copy.start()
            second.append(copy)

    for copy in small:
        copy.wait()
    gain_row = gain_ref[...]
    gain_col = jnp.broadcast_to(gain_row, (128, 128)).T
    basis_t = start_ref[...]

    acc = jnp.zeros((256, 256), F32)
    across = {}
    for a in range(2):
        for rel in range(3):
            first[rel, a].wait_recv()
        if a == 1:
            for piece in range(2):
                for rel, j in ((1, me), (2, sib)):
                    copy = remote(buf.at[j, piece, me], buf.at[j, piece, me], send3.at[rel - 1, piece],
                                  recv3.at[rel - 1, piece], others[rel])
                    copy.start()
                    across[rel, piece] = copy
        flat = buf.at[me, a].reshape(128 * layers, 128)
        for pair in range(layers // 2):
            block = []
            for l in (2 * pair, 2 * pair + 1):
                y = above(*split_two(flat[pl.ds(l, 128, stride=layers), :]))
                parts[me, a * layers + l] = y
                block.append(y)
            both = beside(*block)
            acc = acc + lax.dot_general(both, both, (((1,), (1,)), ((), ())),
                                        preferred_element_type=F32)
    gram_part[...] = (acc[:128, :128] + acc[128:, 128:]) + (acc[:128, 128:] + acc[128:, :128])

    def own_rows(g):
        return pl.ds(pl.multiple_of(g * own, own), own)

    def share(g, c):
        return pl.ds(pl.multiple_of((lax.rem(c, 2) * 4 + g) * (own // 2), own // 2), own // 2)

    def to_group(src, dst, send, recv, g, c):
        return pltpu.make_async_remote_copy(src_ref=src, dst_ref=dst, send_sem=send, recv_sem=recv,
                                            device_id={"per": g, "cells": c}, device_id_type=MESH)

    order = (6, 7, 5, 4, 2, 3, 1)
    mine_only = share(me, my_cell)

    scatter = []
    for rel in order:
        g, c = group[rel]
        copy = to_group(gram_part.at[share(g, c)], scattered.at[rel], rs_send.at[rel],
                        rs_recv.at[rel], g, c)
        copy.start()
        scatter.append(copy)
    relay_a = remote(buf.at[me, :, pl.ds(base, 2)], buf.at[me, :, pl.ds(base, 2)], relay_send.at[0],
                     relay_recv.at[0], sib)
    relay_a.start()
    for copy in scatter:
        copy.wait_recv()
    slots[half] = ((gram_part[mine_only, :] + scattered[1]) + (scattered[2] + scattered[3])) + (
        (scattered[4] + scattered[5]) + (scattered[6] + scattered[7]))

    def broadcast(step):
        other = distant(step)
        return pltpu.make_async_remote_copy(
            src_ref=slots.at[half], dst_ref=slots.at[half], send_sem=bc_send.at[other],
            recv_sem=bc_recv.at[half], device_id={"cells": 2 * other + parity}, device_id_type=MESH)

    def arrival(step):
        other = distant(step)
        return pltpu.make_async_remote_copy(
            src_ref=slots.at[other], dst_ref=slots.at[other], send_sem=bc_send.at[other],
            recv_sem=bc_recv.at[other], device_id={"cells": 2 * other + parity}, device_id_type=MESH)

    def start_broadcast(step, carry):
        broadcast(step).start()
        return carry

    def wait_broadcast(step, carry):
        arrival(step).wait_recv()
        return carry

    def wait_sent(step, carry):
        broadcast(step).wait_send()
        return carry

    lax.fori_loop(1, halves, start_broadcast, 0)

    def relay_across(a):
        for rel in (1, 2):
            across[rel, a].wait_recv()
        place = buf.at[peer, a, pl.ds(base, 2)]
        copy = remote(place, place, relay_send.at[1 + a], relay_recv.at[1 + a], sib)
        copy.start()
        return copy

    def prepare(j, g, pieces=(0, 1)):
        for a in pieces:
            source = buf.at[j, a, g].reshape(own * layers, 128)
            for l in range(layers):
                hi, lo = split_two(source[pl.ds(l, own, stride=layers), :])
                parts[j, a * layers + l, own_rows(g), :] = hi
                parts[j, a * layers + l, pl.ds(pl.multiple_of(128 + g * own, own), own), :] = lo

    for j in (sib, peer, cross):
        prepare(j, me)
    for copy in second:
        copy.wait_recv()
    for j in (sib, peer, cross):
        prepare(j, sib)

    lax.fori_loop(1, halves, wait_broadcast, 0)

    def add(step, total):
        return total + slots[step]

    gram_full[mine_only, :] = lax.fori_loop(1, halves, add, slots[0])
    gather = []
    for rel in order:
        g, c = group[rel]
        copy = to_group(gram_full.at[mine_only], gram_full.at[mine_only], ag_send.at[rel],
                        ag_recv.at[rel], g, c)
        copy.start()
        gather.append(copy)
    for copy in gather:
        copy.wait_recv()

    weights = gram_weights(gram_full[...] * gain_row * gain_col * (1.0 / total_rows))
    basis_t = refine_step(weights, basis_t)
    relay_a.wait_recv()
    for g in (peer, cross):
        prepare(sib, g)
    relays = [relay_across(0)]
    basis_t = refine_step(weights, basis_t)
    for g in (peer, cross):
        prepare(peer, g, (0,))
    for step in range(2, ITERS):
        basis_t = refine_step(weights, basis_t)
    relays.append(relay_across(1))
    proj_ref[...] = outer_of(basis_t)
    hi, lo = split_two(proj_ref[own_rows(me), :] * gain_row)
    weights = above(beside(hi, hi), beside(lo, jnp.zeros_like(lo)))

    for g in (peer, cross):
        prepare(peer, g, (1,))
    relays[0].wait_recv()
    for g in (peer, cross):
        prepare(cross, g, (0,))
    written = []
    for index, j in enumerate((me,) + others):
        if index == 3:
            relays[1].wait_recv()
            for g in (peer, cross):
                prepare(cross, g, (1,))
        for r in range(0, rows, 2):
            target = out_buf.at[j, r // layers].reshape(own * layers, 128)
            l = r % layers
            result = jnp.dot(weights, beside(parts[j, r], parts[j, r + 1]), preferred_element_type=F32)
            result = result[:own] + result[own:]
            target[pl.ds(l, own, stride=layers), :] = result[:, :128]
            target[pl.ds(l + 1, own, stride=layers), :] = result[:, 128:]
            if l + 2 == layers:
                a = r // layers
                copy = pltpu.make_async_copy(out_buf.at[j, a], out.at[:, a, :, lanes(j)],
                                             out_sem.at[index, a])
                copy.start()
                written.append(copy)

    for copy in list(first.values()) + second + list(across.values()) + scatter + gather + [relay_a] + relays:
        copy.wait_send()
    lax.fori_loop(1, halves, wait_sent, 0)
    for copy in written:
        copy.wait()


def per_device(field, period_gain, start_basis):
    cells = lax.axis_size("cells")
    own, _, layers, width = field.shape
    total_rows = 2.0 * layers * width * cells
    any_space = pl.BlockSpec(memory_space=pl.ANY)
    dma = pltpu.SemaphoreType.DMA
    return pl.pallas_call(
        functools.partial(kernel, cells, total_rows),
        out_shape=jax.ShapeDtypeStruct(field.shape, F32),
        in_specs=[pl.BlockSpec(memory_space=pltpu.HBM)] * 3,
        out_specs=any_space,
        scratch_shapes=[
            pltpu.VMEM((4, 2, 4, own, layers, 128), F32),
            pltpu.VMEM((4, 2 * layers, 256, 128), BF16),
            pltpu.VMEM((4, 2, own, layers, 128), F32),
            pltpu.VMEM((1, 128), F32),
            pltpu.VMEM(start_basis.shape[::-1], F32),
            pltpu.VMEM((128, 128), F32),
            pltpu.VMEM((8, own // 2, 128), F32),
            pltpu.VMEM((cells // 2, own // 2, 128), F32),
            pltpu.VMEM((128, 128), F32),
            pltpu.VMEM((128, 128), F32),
            dma((4, 2)), dma((2,)), dma((4, 2)),
            dma((3, 2)), dma((3, 2)),
            dma((3, 2)), dma((3, 2)),
            dma((2, 2)), dma((2, 2)),
            dma((3,)), dma((3,)),
            dma((8,)), dma((8,)),
            dma((cells // 2,)), dma((cells // 2,)),
            dma((8,)), dma((8,)),
        ],
        compiler_params=pltpu.CompilerParams(
            collective_id=0, has_side_effects=True, vmem_limit_bytes=36 * 1024 * 1024),
        name="factor_and_project",
    )(field, period_gain.reshape(1, -1), start_basis.T)


def solution(mesh):
    in_specs = (P("per", None, None, "cells"), P(), P())
    out_specs = P("per", None, None, "cells")
    return jax.shard_map(
        per_device, mesh=mesh, in_specs=in_specs, out_specs=out_specs, check_vma=False
    )
```

```python
import functools
import jax
import jax.numpy as jnp
from jax import lax
from jax.experimental import pallas as pl
from jax.experimental.pallas import tpu as pltpu
from jax.sharding import PartitionSpec as P

ITERS = 3
HIGH = lax.Precision.HIGHEST
MESH = pl.DeviceIdType.MESH
F32 = jnp.float32
BF16 = jnp.bfloat16


def split_two(x):
    hi = x.astype(BF16)
    return hi, (x - hi.astype(F32)).astype(BF16)


def split_three(x):
    first = x.astype(BF16)
    rest = x - first.astype(F32)
    second = rest.astype(BF16)
    return first, second, (rest - second.astype(F32)).astype(BF16)


def beside(*blocks):
    return jnp.concatenate(blocks, axis=1)


def above(*blocks):
    return jnp.concatenate(blocks, axis=0)


def gram_weights(gram):
    first, second, third = split_three(gram)
    return above(beside(first, third), beside(second, jnp.zeros_like(second)))


def inverse_of(x):
    guess = pl.reciprocal(x, approx=True)
    return guess * (2.0 - x * guess)


def eliminate(grown, inner):
    tiles = grown.shape[0] // 8
    width = grown.shape[1]
    x = [grown[8 * t:8 * t + 8] for t in range(tiles)]
    a = [inner[8 * t:8 * t + 8] for t in range(tiles)]
    row_id = lax.broadcasted_iota(jnp.int32, (8, width), 0)
    for t in range(tiles):
        column = {}
        for j in range(8):
            for s in range(t, tiles):
                column[j, s] = jnp.broadcast_to(a[s][:, 8 * t + j:8 * t + j + 1], (8, width))
        pivots = jnp.ones((8, width), F32)
        for j in range(8):
            inverse = inverse_of(jnp.broadcast_to(column[j, t][j:j + 1], (8, width)))
            pivots = jnp.where(row_id == j, column[j, t], pivots)
            factor = {s: column[j, s] * inverse for s in range(t, tiles)}
            factor[t] = jnp.where(row_id > j, factor[t], 0.0)
            later = {i: jnp.broadcast_to(column[i, t][j:j + 1], (8, width)) for i in range(j + 1, 8)}
            x_row = jnp.broadcast_to(x[t][j:j + 1], (8, width))
            a_row = jnp.broadcast_to(a[t][j:j + 1], a[t].shape)
            for s in range(t, tiles):
                for i in range(j + 1, 8):
                    column[i, s] = column[i, s] - factor[s] * later[i]
                x[s] = x[s] - factor[s] * x_row
                if s > t:
                    a[s] = a[s] - factor[s][:, :a_row.shape[1]] * a_row
            if t < tiles - 1:
                a[t] = a[t] - factor[t][:, :a_row.shape[1]] * a_row
        x[t] = x[t] * lax.rsqrt(pivots)
    return above(*x)


def refine_step(weights, basis_t):
    rank, periods = basis_t.shape
    b1, b2, b3 = split_three(basis_t)
    zero = jnp.zeros_like(b1)
    product = jnp.dot(above(beside(b1, b1), beside(b2, b2), beside(b3, zero)), weights,
                      preferred_element_type=F32)
    low, high = product[:, :periods], product[:, periods:]
    grown = low[:rank] + ((low[rank:2 * rank] + high[:rank]) + (low[2 * rank:] + high[rank:2 * rank]))
    g1, g2, g3 = split_three(grown)
    product = lax.dot_general(
        above(beside(g1, g1, g1), beside(g2, g2, zero), beside(g3, zero, zero)),
        beside(g1, g2, g3), (((1,), (1,)), ((), ())), preferred_element_type=F32)
    inner = product[:rank] + (product[rank:2 * rank] + product[2 * rank:])
    return eliminate(grown, inner)


def outer_of(basis_t):
    q1, q2, q3 = split_three(basis_t)
    return lax.dot_general(above(q1, q1, q1, q2, q2, q3), above(q1, q2, q3, q1, q2, q1),
                           (((0,), (0,)), ((), ())), preferred_element_type=F32)


def kernel(cells, total_rows, field, gain_any, start_any, out, buf, parts, out_buf, gain_ref, start_ref, gram_part,
           scattered, slots, gram_full, proj_ref, local_sem, small_sem, out_sem, send1, recv1, send2, recv2, send3, recv3,
           relay_send, relay_recv, rs_send, rs_recv, bc_send, bc_recv, ag_send, ag_recv):
    me = lax.axis_index("per")
    my_cell = lax.axis_index("cells")
    sib = me + 1 - 2 * lax.rem(me, 2)
    peer = lax.rem(me + 2, 4)
    cross = lax.rem(sib + 2, 4)
    base = 2 * (1 - me // 2)
    others = (sib, peer, cross)
    own = field.shape[0]
    layers = field.shape[2]
    rows = 2 * layers

    def lanes(j):
        return pl.ds(pl.multiple_of(j * 128, 128), 128)

    local = {}
    for a in range(2):
        for index, j in ((2, peer), (3, cross), (1, sib), (0, me)):
            copy = pltpu.make_async_copy(field.at[:, a, :, lanes(j)], buf.at[j, a, me],
                                         local_sem.at[index, a])
            copy.start()
            local[index, a] = copy

    small = [pltpu.make_async_copy(gain_any, gain_ref, small_sem.at[0]),
             pltpu.make_async_copy(start_any, start_ref, small_sem.at[1])]
    for copy in small:
        copy.start()

    barrier = pltpu.get_barrier_semaphore()
    parity = lax.rem(my_cell, 2)
    half = my_cell // 2
    halves = cells // 2
    pair_cell = my_cell + 1 - 2 * parity
    group = [(g, c) for c in (my_cell, pair_cell) for g in (me,) + others]
    for g, c in group[1:]:
        pl.semaphore_signal(barrier, inc=1, device_id={"per": g, "cells": c}, device_id_type=MESH)

    def distant(step):
        return lax.rem(half + step, halves)

    def greet(step, carry):
        pl.semaphore_signal(barrier, inc=1, device_id={"cells": 2 * distant(step) + parity},
                            device_id_type=MESH)
        return carry

    lax.fori_loop(1, halves, greet, 0)
    pl.semaphore_wait(barrier, 7 + halves - 1)

    def remote(src, dst, send, recv, other):
        return pltpu.make_async_remote_copy(src_ref=src, dst_ref=dst, send_sem=send, recv_sem=recv,
                                            device_id={"per": other}, device_id_type=MESH)

    first = {}
    for a in range(2):
        for rel in (1, 2, 0):
            other = others[rel]
            local[rel + 1, a].wait()
            copy = remote(buf.at[other, a, me], buf.at[other, a, me],
                          send1.at[rel, a], recv1.at[rel, a], other)
            copy.start()
            first[rel, a] = copy

    second = []
    for index, j in enumerate((me, peer, cross)):
        for a in range(2):
            if index == 0:
                local[0, a].wait()
            copy = remote(buf.at[j, a, me], buf.at[j, a, me], send2.at[index, a], recv2.at[index, a], sib)
            copy.start()
            second.append(copy)

    for copy in small:
        copy.wait()
    gain_row = gain_ref[...]
    gain_col = jnp.broadcast_to(gain_row, (128, 128)).T
    basis_t = start_ref[...]

    acc = jnp.zeros((256, 256), F32)
    for a in range(2):
        for rel in range(3):
            first[rel, a].wait_recv()
        flat = buf.at[me, a].reshape(128 * layers, 128)
        for pair in range(layers // 2):
            block = []
            for l in (2 * pair, 2 * pair + 1):
                y = above(*split_two(flat[pl.ds(l, 128, stride=layers), :]))
                parts[me, a * layers + l] = y
                block.append(y)
            both = beside(*block)
            acc = acc + lax.dot_general(both, both, (((1,), (1,)), ((), ())),
                                        preferred_element_type=F32)
    gram_part[...] = (acc[:128, :128] + acc[128:, 128:]) + (acc[:128, 128:] + acc[128:, :128])

    def own_rows(g):
        return pl.ds(pl.multiple_of(g * own, own), own)

    def share(g, c):
        return pl.ds(pl.multiple_of((lax.rem(c, 2) * 4 + g) * (own // 2), own // 2), own // 2)

    def to_group(src, dst, send, recv, g, c):
        return pltpu.make_async_remote_copy(src_ref=src, dst_ref=dst, send_sem=send, recv_sem=recv,
                                            device_id={"per": g, "cells": c}, device_id_type=MESH)

    order = (6, 7, 5, 4, 2, 3, 1)
    mine_only = share(me, my_cell)

    scatter = []
    for rel in order:
        g, c = group[rel]
        copy = to_group(gram_part.at[share(g, c)], scattered.at[rel], rs_send.at[rel],
                        rs_recv.at[rel], g, c)
        copy.start()
        scatter.append(copy)
    relay_a = remote(buf.at[me, :, pl.ds(base, 2)], buf.at[me, :, pl.ds(base, 2)], relay_send.at[0],
                     relay_recv.at[0], sib)
    relay_a.start()
    for copy in scatter:
        copy.wait_recv()
    slots[half] = ((gram_part[mine_only, :] + scattered[1]) + (scattered[2] + scattered[3])) + (
        (scattered[4] + scattered[5]) + (scattered[6] + scattered[7]))

    def broadcast(step):
        other = distant(step)
        return pltpu.make_async_remote_copy(
            src_ref=slots.at[half], dst_ref=slots.at[half], send_sem=bc_send.at[other],
            recv_sem=bc_recv.at[half], device_id={"cells": 2 * other + parity}, device_id_type=MESH)

    def arrival(step):
        other = distant(step)
        return pltpu.make_async_remote_copy(
            src_ref=slots.at[other], dst_ref=slots.at[other], send_sem=bc_send.at[other],
            recv_sem=bc_recv.at[other], device_id={"cells": 2 * other + parity}, device_id_type=MESH)

    def start_broadcast(step, carry):
        broadcast(step).start()
        return carry

    def wait_broadcast(step, carry):
        arrival(step).wait_recv()
        return carry

    def wait_sent(step, carry):
        broadcast(step).wait_send()
        return carry

    lax.fori_loop(1, halves, start_broadcast, 0)

    pieces = ((0, 0, own // 2), (0, own // 2, own // 2), (1, 0, own))
    across = {}
    for n, (a, first_row, count) in enumerate(pieces):
        for rel, j in ((1, me), (2, sib)):
            place = buf.at[j, a, me, pl.ds(first_row, count)]
            across[rel, n] = remote(place, place, send3.at[rel - 1, n], recv3.at[rel - 1, n], others[rel])

    def start_across(n):
        for rel in (1, 2):
            across[rel, n].start()

    def relay_across(n):
        for rel in (1, 2):
            across[rel, n].wait_recv()
        a, first_row, count = pieces[n]
        place = buf.at[peer, a, pl.ds(base, 2), pl.ds(first_row, count)]
        copy = remote(place, place, relay_send.at[1 + n], relay_recv.at[1 + n], sib)
        copy.start()
        return copy

    start_across(0)

    def prepare(j, g, pieces=(0, 1)):
        for a in pieces:
            source = buf.at[j, a, g].reshape(own * layers, 128)
            for l in range(layers):
                hi, lo = split_two(source[pl.ds(l, own, stride=layers), :])
                parts[j, a * layers + l, own_rows(g), :] = hi
                parts[j, a * layers + l, pl.ds(pl.multiple_of(128 + g * own, own), own), :] = lo

    for j in (sib, peer, cross):
        prepare(j, me)
    for copy in second:
        copy.wait_recv()
    for j in (sib, peer, cross):
        prepare(j, sib)

    lax.fori_loop(1, halves, wait_broadcast, 0)

    def add(step, total):
        return total + slots[step]

    gram_full[mine_only, :] = lax.fori_loop(1, halves, add, slots[0])
    gather = []
    for rel in order:
        g, c = group[rel]
        copy = to_group(gram_full.at[mine_only], gram_full.at[mine_only], ag_send.at[rel],
                        ag_recv.at[rel], g, c)
        copy.start()
        gather.append(copy)
    start_across(1)
    start_across(2)
    for copy in gather:
        copy.wait_recv()

    weights = gram_weights(gram_full[...] * gain_row * gain_col * (1.0 / total_rows))
    basis_t = refine_step(weights, basis_t)
    relay_a.wait_recv()
    for g in (peer, cross):
        prepare(sib, g)
    relays = [relay_across(0)]
    basis_t = refine_step(weights, basis_t)
    relays.append(relay_across(1))
    for g in (peer, cross):
        prepare(peer, g, (0,))
    for step in range(2, ITERS):
        basis_t = refine_step(weights, basis_t)
    proj_ref[...] = outer_of(basis_t)
    hi, lo = split_two(proj_ref[own_rows(me), :] * gain_row)
    weights = above(beside(hi, hi), beside(lo, jnp.zeros_like(lo)))

    written = []
    for index, j in enumerate((me,) + others):
        if index == 2:
            relays.append(relay_across(2))
            for g in (peer, cross):
                prepare(peer, g, (1,))
        if index == 3:
            for copy in relays:
                copy.wait_recv()
            for g in (peer, cross):
                prepare(cross, g)
        for r in range(0, rows, 2):
            target = out_buf.at[j, r // layers].reshape(own * layers, 128)
            l = r % layers
            result = jnp.dot(weights, beside(parts[j, r], parts[j, r + 1]), preferred_element_type=F32)
            result = result[:own] + result[own:]
            target[pl.ds(l, own, stride=layers), :] = result[:, :128]
            target[pl.ds(l + 1, own, stride=layers), :] = result[:, 128:]
            if l + 2 == layers:
                a = r // layers
                copy = pltpu.make_async_copy(out_buf.at[j, a], out.at[:, a, :, lanes(j)],
                                             out_sem.at[index, a])
                copy.start()
                written.append(copy)

    for copy in list(first.values()) + second + list(across.values()) + scatter + gather + [relay_a] + relays:
        copy.wait_send()
    lax.fori_loop(1, halves, wait_sent, 0)
    for copy in written:
        copy.wait()


def hand_over(source, target, sems):
    count = source.shape[0] // 8
    copies = [pltpu.make_async_copy(source.at[pl.ds(i * count, count)], target.at[pl.ds(i * count, count)],
                                    sems.at[i]) for i in range(8)]
    for copy in copies:
        copy.start()
    for copy in copies:
        copy.wait()


def per_device(field, period_gain, start_basis):
    cells = lax.axis_size("cells")
    own, _, layers, width = field.shape
    total_rows = 2.0 * layers * width * cells
    any_space = pl.BlockSpec(memory_space=pl.ANY)
    dma = pltpu.SemaphoreType.DMA
    result = pl.pallas_call(
        functools.partial(kernel, cells, total_rows),
        out_shape=jax.ShapeDtypeStruct(field.shape, F32),
        in_specs=[any_space] * 3,
        out_specs=any_space,
        scratch_shapes=[
            pltpu.VMEM((4, 2, 4, own, layers, 128), F32),
            pltpu.VMEM((4, 2 * layers, 256, 128), BF16),
            pltpu.VMEM((4, 2, own, layers, 128), F32),
            pltpu.VMEM((1, 128), F32),
            pltpu.VMEM(start_basis.shape[::-1], F32),
            pltpu.VMEM((128, 128), F32),
            pltpu.VMEM((8, own // 2, 128), F32),
            pltpu.VMEM((cells // 2, own // 2, 128), F32),
            pltpu.VMEM((128, 128), F32),
            pltpu.VMEM((128, 128), F32),
            dma((4, 2)), dma((2,)), dma((4, 2)),
            dma((3, 2)), dma((3, 2)),
            dma((3, 2)), dma((3, 2)),
            dma((2, 3)), dma((2, 3)),
            dma((4,)), dma((4,)),
            dma((8,)), dma((8,)),
            dma((cells // 2,)), dma((cells // 2,)),
            dma((8,)), dma((8,)),
        ],
        compiler_params=pltpu.CompilerParams(
            collective_id=0, has_side_effects=True, vmem_limit_bytes=56 * 1024 * 1024),
        name="factor_and_project",
    )(field, period_gain.reshape(1, -1), start_basis.T)
    return pl.pallas_call(
        hand_over,
        out_shape=jax.ShapeDtypeStruct(field.shape, F32),
        in_specs=[any_space],
        out_specs=any_space,
        scratch_shapes=[dma((8,))],
        compiler_params=pltpu.CompilerParams(vmem_limit_bytes=56 * 1024 * 1024),
        name="hand_over",
    )(result)


def solution(mesh):
    in_specs = (P("per", None, None, "cells"), P(), P())
    out_specs = P("per", None, None, "cells")
    return jax.shard_map(
        per_device, mesh=mesh, in_specs=in_specs, out_specs=out_specs, check_vma=False
    )
```

```python
import functools
import jax
import jax.numpy as jnp
from jax import lax
from jax.experimental import pallas as pl
from jax.experimental.pallas import tpu as pltpu
from jax.sharding import PartitionSpec as P

ITERS = 3
HIGH = lax.Precision.HIGHEST
MESH = pl.DeviceIdType.MESH
F32 = jnp.float32
BF16 = jnp.bfloat16


def split_two(x):
    hi = x.astype(BF16)
    return hi, (x - hi.astype(F32)).astype(BF16)


def split_three(x):
    first = x.astype(BF16)
    rest = x - first.astype(F32)
    second = rest.astype(BF16)
    return first, second, (rest - second.astype(F32)).astype(BF16)


def beside(*blocks):
    return jnp.concatenate(blocks, axis=1)


def above(*blocks):
    return jnp.concatenate(blocks, axis=0)


def gram_weights(gram):
    first, second, third = split_three(gram)
    return above(beside(first, third), beside(second, jnp.zeros_like(second)))


def inverse_of(x):
    guess = pl.reciprocal(x, approx=True)
    return guess * (2.0 - x * guess)


def eliminate(grown, inner):
    tiles = grown.shape[0] // 8
    width = grown.shape[1]
    x = [grown[8 * t:8 * t + 8] for t in range(tiles)]
    a = [inner[8 * t:8 * t + 8] for t in range(tiles)]
    row_id = lax.broadcasted_iota(jnp.int32, (8, width), 0)
    for t in range(tiles):
        column = {}
        for j in range(8):
            for s in range(t, tiles):
                column[j, s] = jnp.broadcast_to(a[s][:, 8 * t + j:8 * t + j + 1], (8, width))
        pivots = jnp.ones((8, width), F32)
        for j in range(8):
            inverse = inverse_of(jnp.broadcast_to(column[j, t][j:j + 1], (8, width)))
            pivots = jnp.where(row_id == j, column[j, t], pivots)
            factor = {s: column[j, s] * inverse for s in range(t, tiles)}
            factor[t] = jnp.where(row_id > j, factor[t], 0.0)
            later = {i: jnp.broadcast_to(column[i, t][j:j + 1], (8, width)) for i in range(j + 1, 8)}
            x_row = jnp.broadcast_to(x[t][j:j + 1], (8, width))
            a_row = jnp.broadcast_to(a[t][j:j + 1], a[t].shape)
            for s in range(t, tiles):
                for i in range(j + 1, 8):
                    column[i, s] = column[i, s] - factor[s] * later[i]
                x[s] = x[s] - factor[s] * x_row
                if s > t:
                    a[s] = a[s] - factor[s][:, :a_row.shape[1]] * a_row
            if t < tiles - 1:
                a[t] = a[t] - factor[t][:, :a_row.shape[1]] * a_row
        x[t] = x[t] * lax.rsqrt(pivots)
    return above(*x)


def refine_step(weights, basis_t):
    rank, periods = basis_t.shape
    b1, b2, b3 = split_three(basis_t)
    zero = jnp.zeros_like(b1)
    product = jnp.dot(above(beside(b1, b1), beside(b2, b2), beside(b3, zero)), weights,
                      preferred_element_type=F32)
    low, high = product[:, :periods], product[:, periods:]
    grown = low[:rank] + ((low[rank:2 * rank] + high[:rank]) + (low[2 * rank:] + high[rank:2 * rank]))
    g1, g2, g3 = split_three(grown)
    product = lax.dot_general(
        above(beside(g1, g1, g1), beside(g2, g2, zero), beside(g3, zero, zero)),
        beside(g1, g2, g3), (((1,), (1,)), ((), ())), preferred_element_type=F32)
    inner = product[:rank] + (product[rank:2 * rank] + product[2 * rank:])
    return eliminate(grown, inner)


def outer_of(basis_t):
    q1, q2, q3 = split_three(basis_t)
    return lax.dot_general(above(q1, q1, q1, q2, q2, q3), above(q1, q2, q3, q1, q2, q1),
                           (((0,), (0,)), ((), ())), preferred_element_type=F32)


def kernel(cells, total_rows, field, gain_any, start_any, out, buf, parts, out_buf, gain_ref, start_ref, gram_part,
           scattered, slots, gram_full, proj_ref, local_sem, small_sem, out_sem, send1, recv1, send2, recv2, send3, recv3,
           relay_send, relay_recv, rs_send, rs_recv, bc_send, bc_recv, ag_send, ag_recv):
    me = lax.axis_index("per")
    my_cell = lax.axis_index("cells")
    sib = me + 1 - 2 * lax.rem(me, 2)
    peer = lax.rem(me + 2, 4)
    cross = lax.rem(sib + 2, 4)
    base = 2 * (1 - me // 2)
    others = (sib, peer, cross)
    own = field.shape[0]
    layers = field.shape[2]
    rows = 2 * layers

    def lanes(j):
        return pl.ds(pl.multiple_of(j * 128, 128), 128)

    local = {}
    for a in range(2):
        for index, j in ((2, peer), (3, cross), (1, sib), (0, me)):
            copy = pltpu.make_async_copy(field.at[:, a, :, lanes(j)], buf.at[j, a, me],
                                         local_sem.at[index, a])
            copy.start()
            local[index, a] = copy

    small = [pltpu.make_async_copy(gain_any, gain_ref, small_sem.at[0]),
             pltpu.make_async_copy(start_any, start_ref, small_sem.at[1])]
    for copy in small:
        copy.start()

    barrier = pltpu.get_barrier_semaphore()
    parity = lax.rem(my_cell, 2)
    half = my_cell // 2
    halves = cells // 2
    pair_cell = my_cell + 1 - 2 * parity
    group = [(g, c) for c in (my_cell, pair_cell) for g in (me,) + others]
    for g, c in group[1:]:
        pl.semaphore_signal(barrier, inc=1, device_id={"per": g, "cells": c}, device_id_type=MESH)

    def distant(step):
        return lax.rem(half + step, halves)

    def greet(step, carry):
        pl.semaphore_signal(barrier, inc=1, device_id={"cells": 2 * distant(step) + parity},
                            device_id_type=MESH)
        return carry

    lax.fori_loop(1, halves, greet, 0)
    pl.semaphore_wait(barrier, 7 + halves - 1)

    def remote(src, dst, send, recv, other):
        return pltpu.make_async_remote_copy(src_ref=src, dst_ref=dst, send_sem=send, recv_sem=recv,
                                            device_id={"per": other}, device_id_type=MESH)

    first = {}
    for a in range(2):
        for rel in (1, 2, 0):
            other = others[rel]
            local[rel + 1, a].wait()
            copy = remote(buf.at[other, a, me], buf.at[other, a, me],
                          send1.at[rel, a], recv1.at[rel, a], other)
            copy.start()
            first[rel, a] = copy

    for a in range(2):
        local[0, a].wait()

    half_own, eighth = own // 2, own // 8
    pieces = ((0, 0, eighth), (0, eighth, half_own - eighth), (0, half_own, half_own),
              (1, 0, half_own), (1, half_own, half_own))
    across = {}
    for n, (a, first_row, count) in enumerate(pieces):
        for rel, j in ((1, me), (2, sib)):
            place = buf.at[j, a, me, pl.ds(first_row, count)]
            across[rel, n] = remote(place, place, send3.at[rel - 1, n], recv3.at[rel - 1, n], others[rel])

    def start_across(n):
        for rel in (1, 2):
            across[rel, n].start()

    start_across(0)

    second = []
    for index, j in enumerate((me, peer, cross)):
        for a in range(2):
            copy = remote(buf.at[j, a, me], buf.at[j, a, me], send2.at[index, a], recv2.at[index, a], sib)
            copy.start()
            second.append(copy)

    for copy in small:
        copy.wait()
    gain_row = gain_ref[...]
    gain_col = jnp.broadcast_to(gain_row, (128, 128)).T
    basis_t = start_ref[...]

    acc = jnp.zeros((256, 256), F32)
    for a in range(2):
        for rel in range(3):
            first[rel, a].wait_recv()
        flat = buf.at[me, a].reshape(128 * layers, 128)
        for pair in range(layers // 2):
            block = []
            for l in (2 * pair, 2 * pair + 1):
                y = above(*split_two(flat[pl.ds(l, 128, stride=layers), :]))
                parts[me, a * layers + l] = y
                block.append(y)
            both = beside(*block)
            acc = acc + lax.dot_general(both, both, (((1,), (1,)), ((), ())),
                                        preferred_element_type=F32)
    gram_part[...] = (acc[:128, :128] + acc[128:, 128:]) + (acc[:128, 128:] + acc[128:, :128])

    def own_rows(g):
        return pl.ds(pl.multiple_of(g * own, own), own)

    def share(g, c):
        return pl.ds(pl.multiple_of((lax.rem(c, 2) * 4 + g) * (own // 2), own // 2), own // 2)

    def to_group(src, dst, send, recv, g, c):
        return pltpu.make_async_remote_copy(src_ref=src, dst_ref=dst, send_sem=send, recv_sem=recv,
                                            device_id={"per": g, "cells": c}, device_id_type=MESH)

    order = (6, 7, 5, 4, 2, 3, 1)
    mine_only = share(me, my_cell)

    scatter = []
    for rel in order:
        g, c = group[rel]
        copy = to_group(gram_part.at[share(g, c)], scattered.at[rel], rs_send.at[rel],
                        rs_recv.at[rel], g, c)
        copy.start()
        scatter.append(copy)
    relay_a = remote(buf.at[me, :, pl.ds(base, 2)], buf.at[me, :, pl.ds(base, 2)], relay_send.at[0],
                     relay_recv.at[0], sib)
    relay_a.start()
    for copy in scatter:
        copy.wait_recv()
    slots[half] = ((gram_part[mine_only, :] + scattered[1]) + (scattered[2] + scattered[3])) + (
        (scattered[4] + scattered[5]) + (scattered[6] + scattered[7]))

    def broadcast(step):
        other = distant(step)
        return pltpu.make_async_remote_copy(
            src_ref=slots.at[half], dst_ref=slots.at[half], send_sem=bc_send.at[other],
            recv_sem=bc_recv.at[half], device_id={"cells": 2 * other + parity}, device_id_type=MESH)

    def arrival(step):
        other = distant(step)
        return pltpu.make_async_remote_copy(
            src_ref=slots.at[other], dst_ref=slots.at[other], send_sem=bc_send.at[other],
            recv_sem=bc_recv.at[other], device_id={"cells": 2 * other + parity}, device_id_type=MESH)

    def start_broadcast(step, carry):
        broadcast(step).start()
        return carry

    def wait_broadcast(step, carry):
        arrival(step).wait_recv()
        return carry

    def wait_sent(step, carry):
        broadcast(step).wait_send()
        return carry

    lax.fori_loop(1, halves, start_broadcast, 0)

    def relay_across(n, *received):
        for m in received:
            for rel in (1, 2):
                across[rel, m].wait_recv()
        a, first_row = pieces[received[0]][:2]
        count = sum(pieces[m][2] for m in received)
        place = buf.at[peer, a, pl.ds(base, 2), pl.ds(first_row, count)]
        copy = remote(place, place, relay_send.at[1 + n], relay_recv.at[1 + n], sib)
        copy.start()
        return copy

    start_across(1)

    def prepare(j, g, pieces=(0, 1)):
        for a in pieces:
            source = buf.at[j, a, g].reshape(own * layers, 128)
            for l in range(layers):
                hi, lo = split_two(source[pl.ds(l, own, stride=layers), :])
                parts[j, a * layers + l, own_rows(g), :] = hi
                parts[j, a * layers + l, pl.ds(pl.multiple_of(128 + g * own, own), own), :] = lo

    for j in (sib, peer, cross):
        prepare(j, me)
    for copy in second:
        copy.wait_recv()
    for j in (sib, peer, cross):
        prepare(j, sib)

    lax.fori_loop(1, halves, wait_broadcast, 0)

    def add(step, total):
        return total + slots[step]

    gram_full[mine_only, :] = lax.fori_loop(1, halves, add, slots[0])
    gather = []
    for rel in order:
        g, c = group[rel]
        copy = to_group(gram_full.at[mine_only], gram_full.at[mine_only], ag_send.at[rel],
                        ag_recv.at[rel], g, c)
        copy.start()
        gather.append(copy)
    for n in (2, 3, 4):
        start_across(n)
    for copy in gather:
        copy.wait_recv()

    weights = gram_weights(gram_full[...] * gain_row * gain_col * (1.0 / total_rows))
    basis_t = refine_step(weights, basis_t)
    relay_a.wait_recv()
    for g in (peer, cross):
        prepare(sib, g)
    relays = [relay_across(0, 0, 1)]
    basis_t = refine_step(weights, basis_t)
    relays.append(relay_across(1, 2))
    for g in (peer, cross):
        prepare(peer, g, (0,))
    for step in range(2, ITERS):
        basis_t = refine_step(weights, basis_t)
    relays.append(relay_across(2, 3))
    proj_ref[...] = outer_of(basis_t)
    hi, lo = split_two(proj_ref[own_rows(me), :] * gain_row)
    weights = above(beside(hi, hi), beside(lo, jnp.zeros_like(lo)))

    written = []
    for index, j in enumerate((me,) + others):
        if index == 2:
            relays.append(relay_across(3, 4))
            for g in (peer, cross):
                prepare(peer, g, (1,))
        if index == 3:
            for copy in relays:
                copy.wait_recv()
            for g in (peer, cross):
                prepare(cross, g)
        for r in range(0, rows, 2):
            target = out_buf.at[j, r // layers].reshape(own * layers, 128)
            l = r % layers
            result = jnp.dot(weights, beside(parts[j, r], parts[j, r + 1]), preferred_element_type=F32)
            result = result[:own] + result[own:]
            target[pl.ds(l, own, stride=layers), :] = result[:, :128]
            target[pl.ds(l + 1, own, stride=layers), :] = result[:, 128:]
            if l + 2 == layers:
                a = r // layers
                copy = pltpu.make_async_copy(out_buf.at[j, a], out.at[:, a, :, lanes(j)],
                                             out_sem.at[index, a])
                copy.start()
                written.append(copy)

    for copy in list(first.values()) + second + list(across.values()) + scatter + gather + [relay_a] + relays:
        copy.wait_send()
    lax.fori_loop(1, halves, wait_sent, 0)
    for copy in written:
        copy.wait()


def hand_over(source, target, block, sems):
    count = source.shape[0] // 8
    places = [pl.ds(i * count, count) for i in range(8)]
    loads = [pltpu.make_async_copy(source.at[place], block.at[place], sems.at[0, i])
             for i, place in enumerate(places)]
    stores = [pltpu.make_async_copy(block.at[place], target.at[place], sems.at[1, i])
              for i, place in enumerate(places)]
    for copy in loads:
        copy.start()
    for load, store in zip(loads, stores):
        load.wait()
        store.start()
    for copy in stores:
        copy.wait()


def per_device(field, period_gain, start_basis):
    cells = lax.axis_size("cells")
    own, _, layers, width = field.shape
    total_rows = 2.0 * layers * width * cells
    any_space = pl.BlockSpec(memory_space=pl.ANY)
    dma = pltpu.SemaphoreType.DMA
    result = pl.pallas_call(
        functools.partial(kernel, cells, total_rows),
        out_shape=jax.ShapeDtypeStruct(field.shape, F32),
        in_specs=[any_space] * 3,
        out_specs=any_space,
        scratch_shapes=[
            pltpu.VMEM((4, 2, 4, own, layers, 128), F32),
            pltpu.VMEM((4, 2 * layers, 256, 128), BF16),
            pltpu.VMEM((4, 2, own, layers, 128), F32),
            pltpu.VMEM((1, 128), F32),
            pltpu.VMEM(start_basis.shape[::-1], F32),
            pltpu.VMEM((128, 128), F32),
            pltpu.VMEM((8, own // 2, 128), F32),
            pltpu.VMEM((cells // 2, own // 2, 128), F32),
            pltpu.VMEM((128, 128), F32),
            pltpu.VMEM((128, 128), F32),
            dma((4, 2)), dma((2,)), dma((4, 2)),
            dma((3, 2)), dma((3, 2)),
            dma((3, 2)), dma((3, 2)),
            dma((2, 5)), dma((2, 5)),
            dma((5,)), dma((5,)),
            dma((8,)), dma((8,)),
            dma((cells // 2,)), dma((cells // 2,)),
            dma((8,)), dma((8,)),
        ],
        compiler_params=pltpu.CompilerParams(
            collective_id=0, has_side_effects=True, vmem_limit_bytes=56 * 1024 * 1024),
        name="factor_and_project",
    )(field, period_gain.reshape(1, -1), start_basis.T)
    return pl.pallas_call(
        hand_over,
        out_shape=jax.ShapeDtypeStruct(field.shape, F32),
        in_specs=[any_space],
        out_specs=any_space,
        scratch_shapes=[pltpu.VMEM(field.shape, F32), dma((2, 8))],
        compiler_params=pltpu.CompilerParams(vmem_limit_bytes=56 * 1024 * 1024),
        name="hand_over",
    )(result)


def solution(mesh):
    in_specs = (P("per", None, None, "cells"), P(), P())
    out_specs = P("per", None, None, "cells")
    return jax.shard_map(
        per_device, mesh=mesh, in_specs=in_specs, out_specs=out_specs, check_vma=False
    )
```

```python
import functools
import jax
import jax.numpy as jnp
from jax import lax
from jax.experimental import pallas as pl
from jax.experimental.pallas import tpu as pltpu
from jax.sharding import PartitionSpec as P

ITERS = 3
HIGH = lax.Precision.HIGHEST
MESH = pl.DeviceIdType.MESH
F32 = jnp.float32
BF16 = jnp.bfloat16


def split_two(x):
    hi = x.astype(BF16)
    return hi, (x - hi.astype(F32)).astype(BF16)


def split_three(x):
    first = x.astype(BF16)
    rest = x - first.astype(F32)
    second = rest.astype(BF16)
    return first, second, (rest - second.astype(F32)).astype(BF16)


def beside(*blocks):
    return jnp.concatenate(blocks, axis=1)


def above(*blocks):
    return jnp.concatenate(blocks, axis=0)


def gram_weights(gram):
    first, second, third = split_three(gram)
    return above(beside(first, third), beside(second, jnp.zeros_like(second)))


def inverse_of(x):
    guess = pl.reciprocal(x, approx=True)
    return guess * (2.0 - x * guess)


def eliminate(grown, inner):
    tiles = grown.shape[0] // 8
    width = grown.shape[1]
    x = [grown[8 * t:8 * t + 8] for t in range(tiles)]
    a = [inner[8 * t:8 * t + 8] for t in range(tiles)]
    row_id = lax.broadcasted_iota(jnp.int32, (8, width), 0)
    for t in range(tiles):
        column = {}
        for j in range(8):
            for s in range(t, tiles):
                column[j, s] = jnp.broadcast_to(a[s][:, 8 * t + j:8 * t + j + 1], (8, width))
        pivots = jnp.ones((8, width), F32)
        for j in range(8):
            inverse = inverse_of(jnp.broadcast_to(column[j, t][j:j + 1], (8, width)))
            pivots = jnp.where(row_id == j, column[j, t], pivots)
            factor = {s: column[j, s] * inverse for s in range(t, tiles)}
            factor[t] = jnp.where(row_id > j, factor[t], 0.0)
            later = {i: jnp.broadcast_to(column[i, t][j:j + 1], (8, width)) for i in range(j + 1, 8)}
            x_row = jnp.broadcast_to(x[t][j:j + 1], (8, width))
            a_row = jnp.broadcast_to(a[t][j:j + 1], a[t].shape)
            for s in range(t, tiles):
                for i in range(j + 1, 8):
                    column[i, s] = column[i, s] - factor[s] * later[i]
                x[s] = x[s] - factor[s] * x_row
                if s > t:
                    a[s] = a[s] - factor[s][:, :a_row.shape[1]] * a_row
            if t < tiles - 1:
                a[t] = a[t] - factor[t][:, :a_row.shape[1]] * a_row
        x[t] = x[t] * lax.rsqrt(pivots)
    return above(*x)


def refine_step(weights, basis_t):
    rank, periods = basis_t.shape
    b1, b2, b3 = split_three(basis_t)
    zero = jnp.zeros_like(b1)
    product = jnp.dot(above(beside(b1, b1), beside(b2, b2), beside(b3, zero)), weights,
                      preferred_element_type=F32)
    low, high = product[:, :periods], product[:, periods:]
    grown = low[:rank] + ((low[rank:2 * rank] + high[:rank]) + (low[2 * rank:] + high[rank:2 * rank]))
    g1, g2, g3 = split_three(grown)
    product = lax.dot_general(
        above(beside(g1, g1, g1), beside(g2, g2, zero), beside(g3, zero, zero)),
        beside(g1, g2, g3), (((1,), (1,)), ((), ())), preferred_element_type=F32)
    inner = product[:rank] + (product[rank:2 * rank] + product[2 * rank:])
    return eliminate(grown, inner)


def outer_of(basis_t):
    q1, q2, q3 = split_three(basis_t)
    return lax.dot_general(above(q1, q1, q1, q2, q2, q3), above(q1, q2, q3, q1, q2, q1),
                           (((0,), (0,)), ((), ())), preferred_element_type=F32)


def kernel(cells, total_rows, field, gain_any, start_any, out, buf, parts, out_buf, gain_ref, start_ref, gram_part,
           scattered, slots, gram_full, proj_ref, local_sem, small_sem, out_sem, send1, recv1, send2, recv2, send3, recv3,
           relay_send, relay_recv, rs_send, rs_recv, bc_send, bc_recv, ag_send, ag_recv):
    me = lax.axis_index("per")
    my_cell = lax.axis_index("cells")
    sib = me + 1 - 2 * lax.rem(me, 2)
    peer = lax.rem(me + 2, 4)
    cross = lax.rem(sib + 2, 4)
    base = 2 * (1 - me // 2)
    others = (sib, peer, cross)
    own = field.shape[0]
    layers = field.shape[2]
    rows = 2 * layers

    def lanes(j):
        return pl.ds(pl.multiple_of(j * 128, 128), 128)

    local = {}
    for a in range(2):
        for index, j in ((2, peer), (3, cross), (1, sib), (0, me)):
            copy = pltpu.make_async_copy(field.at[:, a, :, lanes(j)], buf.at[j, a, me],
                                         local_sem.at[index, a])
            copy.start()
            local[index, a] = copy

    small = [pltpu.make_async_copy(gain_any, gain_ref, small_sem.at[0]),
             pltpu.make_async_copy(start_any, start_ref, small_sem.at[1])]
    for copy in small:
        copy.start()

    barrier = pltpu.get_barrier_semaphore()
    parity = lax.rem(my_cell, 2)
    half = my_cell // 2
    halves = cells // 2
    pair_cell = my_cell + 1 - 2 * parity
    group = [(g, c) for c in (my_cell, pair_cell) for g in (me,) + others]
    for g, c in group[1:]:
        pl.semaphore_signal(barrier, inc=1, device_id={"per": g, "cells": c}, device_id_type=MESH)

    def distant(step):
        return lax.rem(half + step, halves)

    def greet(step, carry):
        pl.semaphore_signal(barrier, inc=1, device_id={"cells": 2 * distant(step) + parity},
                            device_id_type=MESH)
        return carry

    lax.fori_loop(1, halves, greet, 0)
    pl.semaphore_wait(barrier, 7 + halves - 1)

    def remote(src, dst, send, recv, other):
        return pltpu.make_async_remote_copy(src_ref=src, dst_ref=dst, send_sem=send, recv_sem=recv,
                                            device_id={"per": other}, device_id_type=MESH)

    first = {}
    for a in range(2):
        for rel in (1, 2, 0):
            other = others[rel]
            local[rel + 1, a].wait()
            copy = remote(buf.at[other, a, me], buf.at[other, a, me],
                          send1.at[rel, a], recv1.at[rel, a], other)
            copy.start()
            first[rel, a] = copy

    for a in range(2):
        local[0, a].wait()

    half_own, eighth = own // 2, own // 8
    pieces = ((0, 0, eighth), (0, eighth, half_own - eighth), (0, half_own, half_own),
              (1, 0, half_own), (1, half_own, half_own))
    across = {}
    for n, (a, first_row, count) in enumerate(pieces):
        for rel, j in ((1, me), (2, sib)):
            place = buf.at[j, a, me, pl.ds(first_row, count)]
            across[rel, n] = remote(place, place, send3.at[rel - 1, n], recv3.at[rel - 1, n], others[rel])

    def start_across(n):
        for rel in (1, 2):
            across[rel, n].start()

    start_across(0)

    second = []
    for index, j in enumerate((me, peer, cross)):
        for a in range(2):
            copy = remote(buf.at[j, a, me], buf.at[j, a, me], send2.at[index, a], recv2.at[index, a], sib)
            copy.start()
            second.append(copy)

    for copy in small:
        copy.wait()
    gain_row = gain_ref[...]
    gain_col = jnp.broadcast_to(gain_row, (128, 128)).T
    basis_t = start_ref[...]

    def own_rows(g):
        return pl.ds(pl.multiple_of(g * own, own), own)

    def prepare(j, g, pieces=(0, 1)):
        for a in pieces:
            source = buf.at[j, a, g].reshape(own * layers, 128)
            for l in range(layers):
                hi, lo = split_two(source[pl.ds(l, own, stride=layers), :])
                parts[j, a * layers + l, own_rows(g), :] = hi
                parts[j, a * layers + l, pl.ds(pl.multiple_of(128 + g * own, own), own), :] = lo

    for j in (sib, peer, cross):
        prepare(j, me)
    acc = jnp.zeros((256, 256), F32)
    for a in range(2):
        if a == 1:
            for copy in second:
                copy.wait_recv()
            for j in (sib, peer, cross):
                prepare(j, sib)
        for rel in range(3):
            first[rel, a].wait_recv()
        flat = buf.at[me, a].reshape(128 * layers, 128)
        for pair in range(layers // 2):
            block = []
            for l in (2 * pair, 2 * pair + 1):
                y = above(*split_two(flat[pl.ds(l, 128, stride=layers), :]))
                parts[me, a * layers + l] = y
                block.append(y)
            both = beside(*block)
            acc = acc + lax.dot_general(both, both, (((1,), (1,)), ((), ())),
                                        preferred_element_type=F32)
    gram_part[...] = (acc[:128, :128] + acc[128:, 128:]) + (acc[:128, 128:] + acc[128:, :128])

    def share(g, c):
        return pl.ds(pl.multiple_of((lax.rem(c, 2) * 4 + g) * (own // 2), own // 2), own // 2)

    def to_group(src, dst, send, recv, g, c):
        return pltpu.make_async_remote_copy(src_ref=src, dst_ref=dst, send_sem=send, recv_sem=recv,
                                            device_id={"per": g, "cells": c}, device_id_type=MESH)

    order = (6, 7, 5, 4, 2, 3, 1)
    mine_only = share(me, my_cell)

    scatter = []
    for rel in order:
        g, c = group[rel]
        copy = to_group(gram_part.at[share(g, c)], scattered.at[rel], rs_send.at[rel],
                        rs_recv.at[rel], g, c)
        copy.start()
        scatter.append(copy)
    for copy in scatter:
        copy.wait_recv()
    slots[half] = ((gram_part[mine_only, :] + scattered[1]) + (scattered[2] + scattered[3])) + (
        (scattered[4] + scattered[5]) + (scattered[6] + scattered[7]))

    def broadcast(step):
        other = distant(step)
        return pltpu.make_async_remote_copy(
            src_ref=slots.at[half], dst_ref=slots.at[half], send_sem=bc_send.at[other],
            recv_sem=bc_recv.at[half], device_id={"cells": 2 * other + parity}, device_id_type=MESH)

    def arrival(step):
        other = distant(step)
        return pltpu.make_async_remote_copy(
            src_ref=slots.at[other], dst_ref=slots.at[other], send_sem=bc_send.at[other],
            recv_sem=bc_recv.at[other], device_id={"cells": 2 * other + parity}, device_id_type=MESH)

    def start_broadcast(step, carry):
        broadcast(step).start()
        return carry

    def wait_broadcast(step, carry):
        arrival(step).wait_recv()
        return carry

    def wait_sent(step, carry):
        broadcast(step).wait_send()
        return carry

    lax.fori_loop(1, halves, start_broadcast, 0)
    relay_a = remote(buf.at[me, :, pl.ds(base, 2)], buf.at[me, :, pl.ds(base, 2)], relay_send.at[0],
                     relay_recv.at[0], sib)
    relay_a.start()

    def relay_across(n, *received):
        for m in received:
            for rel in (1, 2):
                across[rel, m].wait_recv()
        a, first_row = pieces[received[0]][:2]
        count = sum(pieces[m][2] for m in received)
        place = buf.at[peer, a, pl.ds(base, 2), pl.ds(first_row, count)]
        copy = remote(place, place, relay_send.at[1 + n], relay_recv.at[1 + n], sib)
        copy.start()
        return copy

    start_across(1)

    lax.fori_loop(1, halves, wait_broadcast, 0)

    def add(step, total):
        return total + slots[step]

    gram_full[mine_only, :] = lax.fori_loop(1, halves, add, slots[0])
    gather = []
    for rel in order:
        g, c = group[rel]
        copy = to_group(gram_full.at[mine_only], gram_full.at[mine_only], ag_send.at[rel],
                        ag_recv.at[rel], g, c)
        copy.start()
        gather.append(copy)
    for n in (2, 3, 4):
        start_across(n)
    relay_a.wait_recv()
    for g in (peer, cross):
        prepare(sib, g)
    for copy in gather:
        copy.wait_recv()

    weights = gram_weights(gram_full[...] * gain_row * gain_col * (1.0 / total_rows))
    basis_t = refine_step(weights, basis_t)
    relays = [relay_across(0, 0, 1)]
    basis_t = refine_step(weights, basis_t)
    relays.append(relay_across(1, 2))
    for g in (peer, cross):
        prepare(peer, g, (0,))
    for step in range(2, ITERS):
        basis_t = refine_step(weights, basis_t)
    relays.append(relay_across(2, 3))
    proj_ref[...] = outer_of(basis_t)
    hi, lo = split_two(proj_ref[own_rows(me), :] * gain_row)
    weights = above(beside(hi, hi), beside(lo, jnp.zeros_like(lo)))

    written = []
    for index, j in enumerate((me,) + others):
        if index == 2:
            relays.append(relay_across(3, 4))
            for g in (peer, cross):
                prepare(peer, g, (1,))
        if index == 3:
            for copy in relays:
                copy.wait_recv()
            for g in (peer, cross):
                prepare(cross, g)
        for r in range(0, rows, 2):
            target = out_buf.at[j, r // layers].reshape(own * layers, 128)
            l = r % layers
            result = jnp.dot(weights, beside(parts[j, r], parts[j, r + 1]), preferred_element_type=F32)
            result = result[:own] + result[own:]
            target[pl.ds(l, own, stride=layers), :] = result[:, :128]
            target[pl.ds(l + 1, own, stride=layers), :] = result[:, 128:]
            if l + 2 == layers:
                a = r // layers
                copy = pltpu.make_async_copy(out_buf.at[j, a], out.at[:, a, :, lanes(j)],
                                             out_sem.at[index, a])
                copy.start()
                written.append(copy)

    for copy in list(first.values()) + second + list(across.values()) + scatter + gather + [relay_a] + relays:
        copy.wait_send()
    lax.fori_loop(1, halves, wait_sent, 0)
    for copy in written:
        copy.wait()


def hand_over(source, target, block, sems):
    count = source.shape[0] // 8
    places = [pl.ds(i * count, count) for i in range(8)]
    loads = [pltpu.make_async_copy(source.at[place], block.at[place], sems.at[0, i])
             for i, place in enumerate(places)]
    stores = [pltpu.make_async_copy(block.at[place], target.at[place], sems.at[1, i])
              for i, place in enumerate(places)]
    for copy in loads:
        copy.start()
    for load, store in zip(loads, stores):
        load.wait()
        store.start()
    for copy in stores:
        copy.wait()


def per_device(field, period_gain, start_basis):
    cells = lax.axis_size("cells")
    own, _, layers, width = field.shape
    total_rows = 2.0 * layers * width * cells
    any_space = pl.BlockSpec(memory_space=pl.ANY)
    dma = pltpu.SemaphoreType.DMA
    result = pl.pallas_call(
        functools.partial(kernel, cells, total_rows),
        out_shape=jax.ShapeDtypeStruct(field.shape, F32),
        in_specs=[any_space] * 3,
        out_specs=any_space,
        scratch_shapes=[
            pltpu.VMEM((4, 2, 4, own, layers, 128), F32),
            pltpu.VMEM((4, 2 * layers, 256, 128), BF16),
            pltpu.VMEM((4, 2, own, layers, 128), F32),
            pltpu.VMEM((1, 128), F32),
            pltpu.VMEM(start_basis.shape[::-1], F32),
            pltpu.VMEM((128, 128), F32),
            pltpu.VMEM((8, own // 2, 128), F32),
            pltpu.VMEM((cells // 2, own // 2, 128), F32),
            pltpu.VMEM((128, 128), F32),
            pltpu.VMEM((128, 128), F32),
            dma((4, 2)), dma((2,)), dma((4, 2)),
            dma((3, 2)), dma((3, 2)),
            dma((3, 2)), dma((3, 2)),
            dma((2, 5)), dma((2, 5)),
            dma((5,)), dma((5,)),
            dma((8,)), dma((8,)),
            dma((cells // 2,)), dma((cells // 2,)),
            dma((8,)), dma((8,)),
        ],
        compiler_params=pltpu.CompilerParams(
            collective_id=0, has_side_effects=True, vmem_limit_bytes=56 * 1024 * 1024),
        name="factor_and_project",
    )(field, period_gain.reshape(1, -1), start_basis.T)
    return pl.pallas_call(
        hand_over,
        out_shape=jax.ShapeDtypeStruct(field.shape, F32),
        in_specs=[any_space],
        out_specs=any_space,
        scratch_shapes=[pltpu.VMEM(field.shape, F32), dma((2, 8))],
        compiler_params=pltpu.CompilerParams(vmem_limit_bytes=56 * 1024 * 1024),
        name="hand_over",
    )(result)


def solution(mesh):
    in_specs = (P("per", None, None, "cells"), P(), P())
    out_specs = P("per", None, None, "cells")
    return jax.shard_map(
        per_device, mesh=mesh, in_specs=in_specs, out_specs=out_specs, check_vma=False
    )
```

```python
import functools
import jax
import jax.numpy as jnp
from jax import lax
from jax.experimental import pallas as pl
from jax.experimental.pallas import tpu as pltpu
from jax.sharding import PartitionSpec as P

ITERS = 3
HIGH = lax.Precision.HIGHEST
MESH = pl.DeviceIdType.MESH
F32 = jnp.float32
BF16 = jnp.bfloat16


def split_two(x):
    hi = x.astype(BF16)
    return hi, (x - hi.astype(F32)).astype(BF16)


def split_three(x):
    first = x.astype(BF16)
    rest = x - first.astype(F32)
    second = rest.astype(BF16)
    return first, second, (rest - second.astype(F32)).astype(BF16)


def beside(*blocks):
    return jnp.concatenate(blocks, axis=1)


def above(*blocks):
    return jnp.concatenate(blocks, axis=0)


def gram_weights(gram):
    first, second, third = split_three(gram)
    return above(beside(first, third), beside(second, jnp.zeros_like(second)))


def inverse_of(x):
    guess = pl.reciprocal(x, approx=True)
    return guess * (2.0 - x * guess)


def eliminate(grown, inner):
    tiles = grown.shape[0] // 8
    width = grown.shape[1]
    x = [grown[8 * t:8 * t + 8] for t in range(tiles)]
    a = [inner[8 * t:8 * t + 8] for t in range(tiles)]
    row_id = lax.broadcasted_iota(jnp.int32, (8, width), 0)
    for t in range(tiles):
        column = {}
        for j in range(8):
            for s in range(t, tiles):
                column[j, s] = jnp.broadcast_to(a[s][:, 8 * t + j:8 * t + j + 1], (8, width))
        pivots = jnp.ones((8, width), F32)
        for j in range(8):
            inverse = inverse_of(jnp.broadcast_to(column[j, t][j:j + 1], (8, width)))
            pivots = jnp.where(row_id == j, column[j, t], pivots)
            factor = {s: column[j, s] * inverse for s in range(t, tiles)}
            factor[t] = jnp.where(row_id > j, factor[t], 0.0)
            later = {i: jnp.broadcast_to(column[i, t][j:j + 1], (8, width)) for i in range(j + 1, 8)}
            x_row = jnp.broadcast_to(x[t][j:j + 1], (8, width))
            a_row = jnp.broadcast_to(a[t][j:j + 1], a[t].shape)
            for s in range(t, tiles):
                for i in range(j + 1, 8):
                    column[i, s] = column[i, s] - factor[s] * later[i]
                x[s] = x[s] - factor[s] * x_row
                if s > t:
                    a[s] = a[s] - factor[s][:, :a_row.shape[1]] * a_row
            if t < tiles - 1:
                a[t] = a[t] - factor[t][:, :a_row.shape[1]] * a_row
        x[t] = x[t] * lax.rsqrt(pivots)
    return above(*x)


def refine_step(weights, basis_t):
    rank, periods = basis_t.shape
    b1, b2, b3 = split_three(basis_t)
    zero = jnp.zeros_like(b1)
    product = jnp.dot(above(beside(b1, b1), beside(b2, b2), beside(b3, zero)), weights,
                      preferred_element_type=F32)
    low, high = product[:, :periods], product[:, periods:]
    grown = low[:rank] + ((low[rank:2 * rank] + high[:rank]) + (low[2 * rank:] + high[rank:2 * rank]))
    g1, g2, g3 = split_three(grown)
    product = lax.dot_general(
        above(beside(g1, g1, g1), beside(g2, g2, zero), beside(g3, zero, zero)),
        beside(g1, g2, g3), (((1,), (1,)), ((), ())), preferred_element_type=F32)
    inner = product[:rank] + (product[rank:2 * rank] + product[2 * rank:])
    return eliminate(grown, inner)


def outer_of(basis_t):
    q1, q2, q3 = split_three(basis_t)
    return lax.dot_general(above(q1, q1, q1, q2, q2, q3), above(q1, q2, q3, q1, q2, q1),
                           (((0,), (0,)), ((), ())), preferred_element_type=F32)


def kernel(cells, total_rows, field, gain_any, start_any, out, buf, parts, out_buf, gain_ref, start_ref, gram_part,
           scattered, slots, gram_full, proj_ref, local_sem, small_sem, out_sem, send1, recv1, send2, recv2, send3, recv3,
           relay_send, relay_recv, rs_send, rs_recv, bc_send, bc_recv, ag_send, ag_recv):
    me = lax.axis_index("per")
    my_cell = lax.axis_index("cells")
    sib = me + 1 - 2 * lax.rem(me, 2)
    peer = lax.rem(me + 2, 4)
    cross = lax.rem(sib + 2, 4)
    base = 2 * (1 - me // 2)
    others = (sib, peer, cross)
    own = field.shape[0]
    layers = field.shape[2]
    rows = 2 * layers

    def lanes(j):
        return pl.ds(pl.multiple_of(j * 128, 128), 128)

    local = {}
    for a in range(2):
        for index, j in ((2, peer), (3, cross), (1, sib), (0, me)):
            copy = pltpu.make_async_copy(field.at[:, a, :, lanes(j)], buf.at[j, a, me],
                                         local_sem.at[index, a])
            copy.start()
            local[index, a] = copy

    small = [pltpu.make_async_copy(gain_any, gain_ref, small_sem.at[0]),
             pltpu.make_async_copy(start_any, start_ref, small_sem.at[1])]
    for copy in small:
        copy.start()

    barrier = pltpu.get_barrier_semaphore()
    parity = lax.rem(my_cell, 2)
    half = my_cell // 2
    halves = cells // 2
    pair_cell = my_cell + 1 - 2 * parity
    group = [(g, c) for c in (my_cell, pair_cell) for g in (me,) + others]
    for g, c in group[1:]:
        pl.semaphore_signal(barrier, inc=1, device_id={"per": g, "cells": c}, device_id_type=MESH)

    def distant(step):
        return lax.rem(half + step, halves)

    def greet(step, carry):
        pl.semaphore_signal(barrier, inc=1, device_id={"cells": 2 * distant(step) + parity},
                            device_id_type=MESH)
        return carry

    lax.fori_loop(1, halves, greet, 0)
    pl.semaphore_wait(barrier, 7 + halves - 1)

    def remote(src, dst, send, recv, other):
        return pltpu.make_async_remote_copy(src_ref=src, dst_ref=dst, send_sem=send, recv_sem=recv,
                                            device_id={"per": other}, device_id_type=MESH)

    first = {}
    for a in range(2):
        for rel in (1, 2, 0):
            other = others[rel]
            local[rel + 1, a].wait()
            copy = remote(buf.at[other, a, me], buf.at[other, a, me],
                          send1.at[rel, a], recv1.at[rel, a], other)
            copy.start()
            first[rel, a] = copy

    for a in range(2):
        local[0, a].wait()

    half_own, eighth = own // 2, own // 8
    pieces = ((0, 0, eighth), (0, eighth, 5 * eighth), (0, 6 * eighth, 2 * eighth),
              (1, 0, half_own), (1, half_own, half_own))
    across = {}
    for n, (a, first_row, count) in enumerate(pieces):
        for rel, j in ((1, me), (2, sib)):
            place = buf.at[j, a, me, pl.ds(first_row, count)]
            across[rel, n] = remote(place, place, send3.at[rel - 1, n], recv3.at[rel - 1, n], others[rel])

    def start_across(n):
        for rel in (1, 2):
            across[rel, n].start()

    start_across(0)

    second = []
    for index, j in enumerate((me, peer, cross)):
        for a in range(2):
            copy = remote(buf.at[j, a, me], buf.at[j, a, me], send2.at[index, a], recv2.at[index, a], sib)
            copy.start()
            second.append(copy)

    for copy in small:
        copy.wait()
    gain_row = gain_ref[...]
    gain_col = jnp.broadcast_to(gain_row, (128, 128)).T
    basis_t = start_ref[...]

    def own_rows(g):
        return pl.ds(pl.multiple_of(g * own, own), own)

    def prepare(j, g, pieces=(0, 1)):
        for a in pieces:
            source = buf.at[j, a, g].reshape(own * layers, 128)
            for l in range(layers):
                hi, lo = split_two(source[pl.ds(l, own, stride=layers), :])
                parts[j, a * layers + l, own_rows(g), :] = hi
                parts[j, a * layers + l, pl.ds(pl.multiple_of(128 + g * own, own), own), :] = lo

    for j in (sib, peer, cross):
        prepare(j, me)
    acc = jnp.zeros((256, 256), F32)
    for a in range(2):
        if a == 1:
            for copy in second:
                copy.wait_recv()
            for j in (sib, peer, cross):
                prepare(j, sib)
        for rel in range(3):
            first[rel, a].wait_recv()
        flat = buf.at[me, a].reshape(128 * layers, 128)
        for pair in range(layers // 2):
            block = []
            for l in (2 * pair, 2 * pair + 1):
                y = above(*split_two(flat[pl.ds(l, 128, stride=layers), :]))
                parts[me, a * layers + l] = y
                block.append(y)
            both = beside(*block)
            acc = acc + lax.dot_general(both, both, (((1,), (1,)), ((), ())),
                                        preferred_element_type=F32)
    gram_part[...] = (acc[:128, :128] + acc[128:, 128:]) + (acc[:128, 128:] + acc[128:, :128])

    def share(g, c):
        return pl.ds(pl.multiple_of((lax.rem(c, 2) * 4 + g) * (own // 2), own // 2), own // 2)

    def to_group(src, dst, send, recv, g, c):
        return pltpu.make_async_remote_copy(src_ref=src, dst_ref=dst, send_sem=send, recv_sem=recv,
                                            device_id={"per": g, "cells": c}, device_id_type=MESH)

    order = (6, 7, 5, 4, 2, 3, 1)
    mine_only = share(me, my_cell)

    scatter = []
    for rel in order:
        g, c = group[rel]
        copy = to_group(gram_part.at[share(g, c)], scattered.at[rel], rs_send.at[rel],
                        rs_recv.at[rel], g, c)
        copy.start()
        scatter.append(copy)
    for copy in scatter:
        copy.wait_recv()
    slots[half] = ((gram_part[mine_only, :] + scattered[1]) + (scattered[2] + scattered[3])) + (
        (scattered[4] + scattered[5]) + (scattered[6] + scattered[7]))

    def broadcast(step):
        other = distant(step)
        return pltpu.make_async_remote_copy(
            src_ref=slots.at[half], dst_ref=slots.at[half], send_sem=bc_send.at[other],
            recv_sem=bc_recv.at[half], device_id={"cells": 2 * other + parity}, device_id_type=MESH)

    def arrival(step):
        other = distant(step)
        return pltpu.make_async_remote_copy(
            src_ref=slots.at[other], dst_ref=slots.at[other], send_sem=bc_send.at[other],
            recv_sem=bc_recv.at[other], device_id={"cells": 2 * other + parity}, device_id_type=MESH)

    def start_broadcast(step, carry):
        broadcast(step).start()
        return carry

    def wait_broadcast(step, carry):
        arrival(step).wait_recv()
        return carry

    def wait_sent(step, carry):
        broadcast(step).wait_send()
        return carry

    lax.fori_loop(1, halves, start_broadcast, 0)
    relay_a = remote(buf.at[me, :, pl.ds(base, 2)], buf.at[me, :, pl.ds(base, 2)], relay_send.at[0],
                     relay_recv.at[0], sib)
    relay_a.start()

    def relay_across(n, *received):
        for m in received:
            for rel in (1, 2):
                across[rel, m].wait_recv()
        a, first_row = pieces[received[0]][:2]
        count = sum(pieces[m][2] for m in received)
        place = buf.at[peer, a, pl.ds(base, 2), pl.ds(first_row, count)]
        copy = remote(place, place, relay_send.at[1 + n], relay_recv.at[1 + n], sib)
        copy.start()
        return copy

    start_across(1)

    lax.fori_loop(1, halves, wait_broadcast, 0)

    def add(step, total):
        return total + slots[step]

    gram_full[mine_only, :] = lax.fori_loop(1, halves, add, slots[0])
    gather = []
    for rel in order:
        g, c = group[rel]
        copy = to_group(gram_full.at[mine_only], gram_full.at[mine_only], ag_send.at[rel],
                        ag_recv.at[rel], g, c)
        copy.start()
        gather.append(copy)
    for n in (2, 3, 4):
        start_across(n)
    relay_a.wait_recv()
    for g in (peer, cross):
        prepare(sib, g)
    for copy in gather:
        copy.wait_recv()

    weights = gram_weights(gram_full[...] * gain_row * gain_col * (1.0 / total_rows))
    basis_t = refine_step(weights, basis_t)
    relays = [relay_across(0, 0, 1)]
    basis_t = refine_step(weights, basis_t)
    relays.append(relay_across(1, 2))
    for g in (peer, cross):
        prepare(peer, g, (0,))
    for step in range(2, ITERS):
        basis_t = refine_step(weights, basis_t)
    relays.append(relay_across(2, 3))
    proj_ref[...] = outer_of(basis_t)
    hi, lo = split_two(proj_ref[own_rows(me), :] * gain_row)
    weights = above(beside(hi, hi), beside(lo, jnp.zeros_like(lo)))

    written = []
    for index, j in enumerate((me,) + others):
        if index == 2:
            relays.append(relay_across(3, 4))
            for g in (peer, cross):
                prepare(peer, g, (1,))
        if index == 3:
            for copy in relays:
                copy.wait_recv()
            for g in (peer, cross):
                prepare(cross, g)
        for r in range(0, rows, 2):
            target = out_buf.at[j, r // layers].reshape(own * layers, 128)
            l = r % layers
            result = jnp.dot(weights, beside(parts[j, r], parts[j, r + 1]), preferred_element_type=F32)
            result = result[:own] + result[own:]
            target[pl.ds(l, own, stride=layers), :] = result[:, :128]
            target[pl.ds(l + 1, own, stride=layers), :] = result[:, 128:]
            if l + 2 == layers:
                a = r // layers
                copy = pltpu.make_async_copy(out_buf.at[j, a], out.at[:, a, :, lanes(j)],
                                             out_sem.at[index, a])
                copy.start()
                written.append(copy)

    for copy in list(first.values()) + second + list(across.values()) + scatter + gather + [relay_a] + relays:
        copy.wait_send()
    lax.fori_loop(1, halves, wait_sent, 0)
    for copy in written:
        copy.wait()


def hand_over(source, target, block, sems):
    count = source.shape[0] // 8
    places = [pl.ds(i * count, count) for i in range(8)]
    loads = [pltpu.make_async_copy(source.at[place], block.at[place], sems.at[0, i])
             for i, place in enumerate(places)]
    stores = [pltpu.make_async_copy(block.at[place], target.at[place], sems.at[1, i])
              for i, place in enumerate(places)]
    for copy in loads:
        copy.start()
    for load, store in zip(loads, stores):
        load.wait()
        store.start()
    for copy in stores:
        copy.wait()


def per_device(field, period_gain, start_basis):
    cells = lax.axis_size("cells")
    own, _, layers, width = field.shape
    total_rows = 2.0 * layers * width * cells
    any_space = pl.BlockSpec(memory_space=pl.ANY)
    dma = pltpu.SemaphoreType.DMA
    result = pl.pallas_call(
        functools.partial(kernel, cells, total_rows),
        out_shape=jax.ShapeDtypeStruct(field.shape, F32),
        in_specs=[any_space] * 3,
        out_specs=any_space,
        scratch_shapes=[
            pltpu.VMEM((4, 2, 4, own, layers, 128), F32),
            pltpu.VMEM((4, 2 * layers, 256, 128), BF16),
            pltpu.VMEM((4, 2, own, layers, 128), F32),
            pltpu.VMEM((1, 128), F32),
            pltpu.VMEM(start_basis.shape[::-1], F32),
            pltpu.VMEM((128, 128), F32),
            pltpu.VMEM((8, own // 2, 128), F32),
            pltpu.VMEM((cells // 2, own // 2, 128), F32),
            pltpu.VMEM((128, 128), F32),
            pltpu.VMEM((128, 128), F32),
            dma((4, 2)), dma((2,)), dma((4, 2)),
            dma((3, 2)), dma((3, 2)),
            dma((3, 2)), dma((3, 2)),
            dma((2, 5)), dma((2, 5)),
            dma((5,)), dma((5,)),
            dma((8,)), dma((8,)),
            dma((cells // 2,)), dma((cells // 2,)),
            dma((8,)), dma((8,)),
        ],
        compiler_params=pltpu.CompilerParams(
            collective_id=0, has_side_effects=True, vmem_limit_bytes=56 * 1024 * 1024),
        name="factor_and_project",
    )(field, period_gain.reshape(1, -1), start_basis.T)
    return pl.pallas_call(
        hand_over,
        out_shape=jax.ShapeDtypeStruct(field.shape, F32),
        in_specs=[any_space],
        out_specs=any_space,
        scratch_shapes=[pltpu.VMEM(field.shape, F32), dma((2, 8))],
        compiler_params=pltpu.CompilerParams(vmem_limit_bytes=56 * 1024 * 1024),
        name="hand_over",
    )(result)


def solution(mesh):
    in_specs = (P("per", None, None, "cells"), P(), P())
    out_specs = P("per", None, None, "cells")
    return jax.shard_map(
        per_device, mesh=mesh, in_specs=in_specs, out_specs=out_specs, check_vma=False
    )
```
